256 devices in a mesh: row: 16 (over x_lo, z), col: 16 (over x_hi, y, core).
Axes of the slice: x: 4 (x_hi: 2, x_lo: 2; x = x_hi * 2 + x_lo), y: 4, z: 8, core: 2. Of those that a mesh axis runs over, the one named last changes fastest.
Arguments:
- points: bfloat16 [96, 1024, 1024], P('row', 'col')
- targets: bfloat16 [96, 1024, 1000], P('row', 'col'), may hold values from -6 to 6
- coeffs: float32 [96, 1024, 1000], P('row', 'col'), may hold values from -0.25 to 0.25
- block_inverse: float32 [96, 1024, 1024], P('row', 'col'), as said below
- block_order: int32 [96], replicated, may hold values from 0 to 95, each once
Outputs:
- coeffs_out: float32 [96, 1024, 1000], P('row', 'col')
The draws below stay inside these ranges and needn't reach their ends.
Inputs may be any that keep to these rules, and one draw needn't show every extreme that they name: block_inverse[b] is the float32 inverse of the exact Gaussian kernel matrix of block b's points (as in the reference program) plus the identity.
All inputs are finite; a program needn't handle non-finite values.
Results may differ from the reference program's by a relative error of at most 0.0003.
Values may be sent and summed in bfloat16 or wider, within the bound.
A program may use at most 64 MiB of HBM per device.

```python
import jax
import jax.numpy as jnp
from jax import lax

F = 1024
C = 1000
BS = 1024
STEPS = 2
NB = 96


latent_width = 16


ridge_weight = 1.0


def make_points(key):
    latent = jax.random.normal(jax.random.fold_in(key, 11), (NB, BS, latent_width), jnp.float32)
    mixing = jax.random.normal(jax.random.fold_in(key, 12), (latent_width, F), jnp.float32)
    noise = 1.0 * jax.random.normal(jax.random.fold_in(key, 13), (NB, BS, F), jnp.float32)
    return (0.25 * jnp.einsum('nbl,lf->nbf', latent, mixing) + noise).astype(jnp.bfloat16)


def draw_points(key, part):
    return make_points(key)


def draw_block_inverse(key, part):
    rounded = make_points(key).astype(jnp.float32)

    def invert(block_points):
        squares = jnp.sum(block_points * block_points, axis=1)
        inner = jnp.dot(block_points, block_points.T, precision=lax.Precision.HIGHEST)
        distance = squares[:, None] + squares[None, :] - 2.0 * inner
        kernel = jnp.exp(-distance * (0.5 / F))
        return jnp.linalg.inv(kernel + ridge_weight * jnp.eye(BS, dtype=jnp.float32))
    return lax.map(invert, rounded)


def level_of(own_key, shape, split, low, top_value):
    def one(position, parts):
        steps = jax.random.uniform(jax.random.fold_in(jax.random.fold_in(own_key, 6), position), (parts,), jnp.float32, low / len(split), top_value / len(split))
        return jnp.repeat(jnp.exp(steps), shape[position] // parts).reshape((-1,) + (1,) * (len(shape) - position - 1))

    gain = one(*split[0])
    for cut in split[1:]:
        gain = gain * one(*cut)
    return gain


def gaussian(key, extent, width, limit, pieces=(), held_as=jnp.bfloat16):
    factor_of = level_of(key, extent, pieces, -0.22, 0.18) if pieces else 1.0
    values = jax.random.normal(key, extent, jnp.float32) * width * factor_of
    return jnp.minimum(jnp.maximum(values, -limit), limit).astype(held_as)


def setup_inputs(seed: int = 0) -> dict:
    seeds = jax.random.split(jax.random.key(seed), 6)
    return {
        "points": draw_points(jax.random.fold_in(seeds[5], 71), 0),
        "targets": gaussian(seeds[1], (NB, BS, C), 1.0, 6.0, ((0, 16), (1, 16))),
        "coeffs": gaussian(seeds[2], (NB, BS, C), (6.0 / (NB * BS) ** 0.5), 0.25, ((0, 16), (1, 16)), jnp.float32),
        "block_inverse": draw_block_inverse(jax.random.fold_in(seeds[5], 71), 0),
        "block_order": jax.random.permutation(seeds[4], NB).astype(jnp.int32),
    }


ridge_weight = 1.0

def kernel_tile(left_points, right_points):
    left_wide = left_points.astype(jnp.float32)
    right_wide = right_points.astype(jnp.float32)
    inner = lax.dot_general(left_points.astype(jnp.float32), right_points.astype(jnp.float32), (((1,), (1,)), ((), ())), preferred_element_type=jnp.float32)
    distance = jnp.sum(left_wide * left_wide, axis=1)[:, None] + jnp.sum(right_wide * right_wide, axis=1)[None, :] - 2.0 * inner
    return jnp.exp(-distance * (0.5 / left_points.shape[1]))

def reference(points, targets, coeffs, block_inverse, block_order):
    current = coeffs
    for sweep_step in range(STEPS):
        block_id = block_order[sweep_step].astype(jnp.int32)
        active = lax.dynamic_index_in_dim(points, block_id, 0, keepdims=False)

        def accumulate(summed, block_pair):
            other_points, other_coeffs = block_pair
            return (summed + jnp.dot(kernel_tile(active, other_points).astype(jnp.float32), other_coeffs.astype(jnp.float32), precision=lax.Precision.HIGHEST, preferred_element_type=jnp.float32), None)
        summed, unused = lax.scan(accumulate, jnp.zeros((BS, C), jnp.float32), (points, current))
        previous = lax.dynamic_index_in_dim(current, block_id, 0, keepdims=False)
        wanted = lax.dynamic_index_in_dim(targets, block_id, 0, keepdims=False).astype(jnp.float32)
        residual = wanted - summed - ridge_weight * previous
        inverse_block = lax.dynamic_index_in_dim(block_inverse, block_id, 0, keepdims=False)
        refreshed = previous + jnp.dot(inverse_block.astype(jnp.float32), residual.astype(jnp.float32), precision=lax.Precision.HIGHEST, preferred_element_type=jnp.float32)
        current = lax.dynamic_update_index_in_dim(current, refreshed, block_id, 0)
    return current
```

```python
import functools

import jax
import jax.numpy as jnp
from jax import lax
from jax.experimental import pallas as pl
from jax.experimental.pallas import tpu as pltpu
from jax.sharding import PartitionSpec as P

MESH = pl.DeviceIdType.MESH
ANY = pl.BlockSpec(memory_space=pl.ANY)
VMEM = pl.BlockSpec(memory_space=pltpu.VMEM)
DMA = pltpu.SemaphoreType.DMA

ridge_weight = 1.0


def place():
    row, col = lax.axis_index("row"), lax.axis_index("col")
    return col // 8, row // 8, (col // 2) % 4, row % 8, col % 2


def device(x, y, z, core):
    return (x % 2) * 8 + z, (x // 2) * 8 + y * 2 + core


class Group:
    def __init__(self, kind):
        x_hi, x_lo, y, z, core = place()
        row, col = lax.axis_index("row"), lax.axis_index("col")
        x = x_hi * 2 + x_lo
        self.size, self.me, self.at = {
            "row": (16, row, lambda i: (i, col)),
            "col": (16, col, lambda i: (row, i)),
            "x": (4, x, lambda i: device(i, y, z, core)),
            "y": (4, y, lambda i: device(x, i, z, core)),
            "z": (8, z, lambda i: device(x, y, i, core)),
            "core": (2, core, lambda i: device(x, y, z, i)),
        }[kind]

    def after(self, step):
        return lax.rem(self.me + step, self.size)

    def before(self, step):
        return lax.rem(self.me + self.size - step, self.size)


def greet(groups):
    barrier = pltpu.get_barrier_semaphore()
    for group in groups:
        for step in range(1, group.size):
            pl.semaphore_signal(barrier, inc=1, device_id=group.at(group.after(step)), device_id_type=MESH)
    pl.semaphore_wait(barrier, sum(group.size - 1 for group in groups))


def send_all(group, source, target, send_sem, recv_sem):
    copies = []
    for step in range(1, group.size):
        to = group.after(step)
        out = pltpu.make_async_remote_copy(
            src_ref=source(to), dst_ref=target(group.me, step), send_sem=send_sem(step), recv_sem=recv_sem(step),
            device_id=group.at(to), device_id_type=MESH)
        out.start()
        back = pltpu.make_async_remote_copy(
            src_ref=source(to), dst_ref=target(group.before(step), step), send_sem=send_sem(step),
            recv_sem=recv_sem(step), device_id=group.at(to), device_id_type=MESH)
        copies.append((out, back))
    return copies


def arrived(copies):
    for _, back in copies:
        back.wait_recv()


def sent(copies):
    for out, _ in copies:
        out.wait_send()


def exchange_start(group, mode, source, target, send_sems, recv_sems, own_sem):
    pick = (lambda i: source.at[i]) if mode == "each" else (lambda i: source)
    own = pltpu.make_async_copy(pick(group.me), target.at[group.me], own_sem)
    own.start()
    copies = send_all(group, pick, lambda i, step: target.at[i], lambda s: send_sems.at[s - 1], lambda s: recv_sems.at[s - 1])
    return own, copies


def exchange_wait(handle):
    own, copies = handle
    own.wait()
    arrived(copies)
    sent(copies)


def exchange_kernel(plan, *refs):
    count = len(plan)
    sources, targets = refs[:count], refs[count:2 * count]
    send_sems, recv_sems, own_sems = refs[2 * count:]
    groups = {kind: Group(kind) for kind, _ in plan}
    greet(list(groups.values()))
    handles = [
        exchange_start(groups[kind], mode, sources[i], targets[i], send_sems.at[i], recv_sems.at[i], own_sems.at[i])
        for i, (kind, mode) in enumerate(plan)
    ]
    for handle in handles:
        exchange_wait(handle)


def exchange(arrays, plan, collective_id):
    shapes = [a.shape if mode == "each" else (16, *a.shape) for a, (_, mode) in zip(arrays, plan)]
    return pl.pallas_call(
        functools.partial(exchange_kernel, tuple(plan)),
        out_shape=[jax.ShapeDtypeStruct(s, a.dtype) for s, a in zip(shapes, arrays)],
        in_specs=[ANY] * len(arrays),
        out_specs=[ANY] * len(arrays),
        scratch_shapes=[DMA((len(arrays), 15)), DMA((len(arrays), 15)), DMA((len(arrays),))],
        compiler_params=pltpu.CompilerParams(collective_id=collective_id, has_side_effects=True),
    )(*arrays)


def gather_kernel(chunk, full, send_sems, recv_sems, own_sem):
    x_hi, x_lo, y, z, core = place()
    gx, gy, gz, gc = Group("x"), Group("y"), Group("z"), Group("core")
    greet([gx, gy, gz, gc])

    def piece(i):
        quarter, lanes = i // 2, i % 2
        return full.at[core, x_hi, y, x_lo, quarter // 2, pl.ds(pl.multiple_of((quarter % 2) * 16, 16), 16),
                       pl.ds(pl.multiple_of(lanes * 512, 512), 512)]

    def sems(base):
        return (lambda s: send_sems.at[base + s - 1]), (lambda s: recv_sems.at[base + s - 1])

    own = pltpu.make_async_copy(chunk, piece(z), own_sem)
    own.start()
    along_z = send_all(gz, lambda i: chunk, lambda i, s: piece(i), *sems(0))
    own.wait()
    arrived(along_z)
    x_first = send_all(gx, lambda i: full.at[core, x_hi, y, x_lo, 0], lambda i, s: full.at[core, i // 2, y, i % 2, 0], *sems(7))
    y_first = send_all(gy, lambda i: full.at[core, x_hi, y, x_lo, 1], lambda i, s: full.at[core, x_hi, i, x_lo, 1], *sems(10))
    arrived(x_first)
    y_last = send_all(gy, lambda i: full.at[core, :, y, :, 0], lambda i, s: full.at[core, :, i, :, 0], *sems(13))
    arrived(y_first)
    x_last = send_all(gx, lambda i: full.at[core, x_hi, :, x_lo, 1], lambda i, s: full.at[core, i // 2, :, i % 2, 1], *sems(16))
    arrived(y_last)
    across_0 = send_all(gc, lambda i: full.at[core, :, :, :, 0], lambda i, s: full.at[i, :, :, :, 0], *sems(19))
    arrived(x_last)
    across_1 = send_all(gc, lambda i: full.at[core, :, :, :, 1], lambda i, s: full.at[i, :, :, :, 1], *sems(20))
    arrived(across_0)
    arrived(across_1)
    for copies in (along_z, x_first, y_first, y_last, x_last, across_0, across_1):
        sent(copies)


def gather_points(chunk, collective_id):
    return pl.pallas_call(
        gather_kernel,
        out_shape=jax.ShapeDtypeStruct((2, 2, 4, 2, 2, 32, 1024), chunk.dtype),
        in_specs=[ANY],
        out_specs=ANY,
        scratch_shapes=[DMA((21,)), DMA((21,)), DMA],
        compiler_params=pltpu.CompilerParams(collective_id=collective_id, has_side_effects=True),
    )(chunk)


def reduce_kernel(parts, inverse, wanted, total, inverse_out, wanted_out, held, core_in, x_in, y_in, x_sum, y_sum, y_in_2,
                  x_in_2, z_sum, z_in, send_sems, recv_sems, own_sem, more_send, more_recv, more_own):
    x_hi, x_lo, y, z, core = place()
    gx, gy, gz, gc, gr = Group("x"), Group("y"), Group("z"), Group("core"), Group("row")
    greet([gx, gy, gz, gc, gr])

    def sems(base):
        return (lambda s: send_sems.at[base + s - 1]), (lambda s: recv_sems.at[base + s - 1])

    across = send_all(gc, lambda i: parts.at[i], lambda i, s: core_in, *sems(0))
    own = pltpu.make_async_copy(parts.at[core], held, own_sem)
    own.start()
    more = [
        exchange_start(gr, "each", inverse, inverse_out, more_send.at[0], more_recv.at[0], more_own.at[0]),
        exchange_start(gr, "each", wanted, wanted_out, more_send.at[1], more_recv.at[1], more_own.at[1]),
    ]
    own.wait()
    arrived(across)

    def add(i, carry):
        held[i // 4, i % 4] += core_in[i // 4, i % 4]
        return carry

    lax.fori_loop(0, 8, add, 0)
    x_first = send_all(gx, lambda i: held.at[i // 2, :, i % 2, 0], lambda i, s: x_in.at[s - 1], *sems(1))
    y_first = send_all(gy, lambda i: held.at[:, i, :, 1], lambda i, s: y_in.at[s - 1], *sems(4))
    arrived(x_first)
    x_sum[...] = held[x_hi, :, x_lo, 0] + x_in[0] + x_in[1] + x_in[2]
    y_last = send_all(gy, lambda i: x_sum.at[i], lambda i, s: y_in_2.at[s - 1], *sems(7))
    arrived(y_first)
    y_sum[...] = held[:, y, :, 1] + y_in[0] + y_in[1] + y_in[2]
    x_last = send_all(gx, lambda i: y_sum.at[i // 2, i % 2], lambda i, s: x_in_2.at[s - 1], *sems(10))
    arrived(y_last)
    z_sum[0] = x_sum[y] + y_in_2[0] + y_in_2[1] + y_in_2[2]
    arrived(x_last)
    z_sum[1] = y_sum[x_hi, x_lo] + x_in_2[0] + x_in_2[1] + x_in_2[2]

    def slab(i):
        return z_sum.at[i // 4, pl.ds(pl.multiple_of((i % 4) * 64, 64), 64)]

    along_z = send_all(gz, slab, lambda i, s: z_in.at[s - 1], *sems(13))
    arrived(along_z)
    result = z_sum[z // 4, pl.ds(pl.multiple_of((z % 4) * 64, 64), 64)]
    for i in range(7):
        result += z_in[i]
    total[...] = result
    for copies in (across, x_first, y_first, y_last, x_last, along_z):
        sent(copies)
    for handle in more:
        exchange_wait(handle)


def reduce_parts(parts, inverse, wanted, collective_id):
    f32 = jnp.float32
    return pl.pallas_call(
        reduce_kernel,
        out_shape=[jax.ShapeDtypeStruct((64, 128), f32), jax.ShapeDtypeStruct(inverse.shape, f32),
                   jax.ShapeDtypeStruct(wanted.shape, f32)],
        in_specs=[ANY, ANY, ANY],
        out_specs=[VMEM, ANY, ANY],
        scratch_shapes=[
            pltpu.VMEM((2, 4, 2, 2, 256, 128), f32),
            pltpu.VMEM((2, 4, 2, 2, 256, 128), f32),
            pltpu.VMEM((3, 4, 256, 128), f32),
            pltpu.VMEM((3, 2, 2, 256, 128), f32),
            pltpu.VMEM((4, 256, 128), f32),
            pltpu.VMEM((2, 2, 256, 128), f32),
            pltpu.VMEM((3, 256, 128), f32),
            pltpu.VMEM((3, 256, 128), f32),
            pltpu.VMEM((2, 256, 128), f32),
            pltpu.VMEM((7, 64, 128), f32),
            DMA((20,)), DMA((20,)), DMA, DMA((2, 15)), DMA((2, 15)), DMA((2,)),
        ],
        compiler_params=pltpu.CompilerParams(collective_id=collective_id, has_side_effects=True, vmem_limit_bytes=40 * 2**20),
    )(parts, inverse, wanted)


def squares(points):
    wide = points.astype(jnp.float32)
    return jnp.sum(wide * wide, axis=-1)


def kern(left, right):
    inner = lax.dot_general(left, right, (((1,), (1,)), ((), ())), preferred_element_type=jnp.float32)
    distance = squares(left)[:, None] + squares(right)[None, :] - 2.0 * inner
    return jnp.exp(-distance * (0.5 / left.shape[1]))


def product(left, right, contract):
    return lax.dot_general(left, right, (contract, ((), ())), precision=lax.Precision.HIGH,
                           preferred_element_type=jnp.float32)


def on_device(points, targets, coeffs, block_inverse, block_order):
    blocks_here, per_col, features = points.shape
    classes = targets.shape[2]
    f32 = jnp.float32
    my_row = lax.axis_index("row")
    x_lo = my_row // 8
    ids = [block_order[0], block_order[1]]
    local = [b % blocks_here for b in ids]
    owner = [b // blocks_here for b in ids]

    def pick(array, step):
        return lax.dynamic_index_in_dim(array, local[step], 0, keepdims=False)

    def both(array):
        return jnp.stack([pick(array, 0), pick(array, 1)])

    own_points = both(points).reshape(2, 4, 16, 2, 512).transpose(0, 1, 3, 2, 4).reshape(16, 16, 512)
    (offers,) = exchange([own_points], [("row", "each")], 0)
    my_owner = jnp.where(x_lo == 0, owner[0], owner[1])
    chunk = lax.dynamic_index_in_dim(offers, my_owner, 0, keepdims=False)
    active = gather_points(chunk, 1)

    inverse_offer = both(block_inverse).reshape(16, 8, 1024)
    previous = both(coeffs)
    need = both(targets).astype(f32) - ridge_weight * previous
    need = jnp.pad(need, ((0, 0), (0, 0), (0, 1024 - classes)))
    wanted_offer = need.transpose(2, 0, 1).reshape(16, 64, 128)

    flat_points = points.reshape(blocks_here * per_col, features)
    flat_coeffs = jnp.pad(coeffs.reshape(blocks_here * per_col, classes), ((0, 0), (0, 1024 - classes)))
    tile = kern(active.reshape(2048, features), flat_points)
    parts = product(flat_coeffs, tile, ((0,), (1,)))
    parts = parts.reshape(1024, 16, 128).transpose(1, 0, 2).reshape(2, 2, 4, 2, 2, 256, 128)
    total, inverse_got, wanted_got = reduce_parts(parts, inverse_offer, wanted_offer, 2)

    inverse_chunk = lax.dynamic_index_in_dim(inverse_got, my_owner, 0, keepdims=False)
    wanted = jnp.concatenate([
        lax.dynamic_index_in_dim(wanted_got, owner[0], 0, keepdims=False)[:, :64],
        lax.dynamic_index_in_dim(wanted_got, owner[1], 0, keepdims=False)[:, 64:],
    ], axis=1)
    residual = wanted - total
    residual_all, inverse_all = exchange([residual, inverse_chunk], [("col", "all"), ("row", "all")], 3)
    inverse = inverse_all.reshape(2, 64, 1024)
    residual_all = residual_all.reshape(16, 64, 2, 64).transpose(2, 1, 0, 3).reshape(2, 64, 1024)

    delta_1 = product(residual_all[0], inverse[0], ((1,), (1,)))
    (delta_all,) = exchange([jnp.pad(delta_1, ((0, 0), (0, 64)))], [("col", "all")], 4)
    delta_all = delta_all[:, :, :64].transpose(1, 0, 2).reshape(64, 1024)
    ordered = active.transpose(3, 1, 2, 0, 4, 5, 6).reshape(2, 1024, features)
    between = kern(ordered[1], ordered[0])
    residual_2 = residual_all[1] - product(delta_all, between, ((1,), (1,)))
    delta_2 = product(residual_2, inverse[1], ((1,), (1,)))
    (deltas,) = exchange([jnp.concatenate([delta_1, delta_2], axis=1)], [("row", "all")], 5)
    deltas = deltas.reshape(1024, 2, 64).transpose(1, 2, 0)[:, :, :classes]

    current = coeffs
    for step in range(2):
        before = lax.dynamic_index_in_dim(current, local[step], 0, keepdims=False)
        updated = jnp.where(my_row == owner[step], before + deltas[step], before)
        current = lax.dynamic_update_index_in_dim(current, updated, local[step], 0)
    return current


def solution(mesh):
    placed = (
        P("row", "col", None),
        P("row", "col", None),
        P("row", "col", None),
        P("row", "col", None),
        P(),
    )
    return jax.shard_map(
        on_device, mesh=mesh, in_specs=placed, out_specs=P("row", "col", None), check_vma=False
    )
```

```python
import functools

import jax
import jax.numpy as jnp
from jax import lax
from jax.experimental import pallas as pl
from jax.experimental.pallas import tpu as pltpu
from jax.sharding import PartitionSpec as P

MESH = pl.DeviceIdType.MESH
ANY = pl.BlockSpec(memory_space=pl.ANY)
VMEM = pl.BlockSpec(memory_space=pltpu.VMEM)
DMA = pltpu.SemaphoreType.DMA

ridge_weight = 1.0


def place():
    row, col = lax.axis_index("row"), lax.axis_index("col")
    return col // 8, row // 8, (col // 2) % 4, row % 8, col % 2


def device(x, y, z, core):
    return (x % 2) * 8 + z, (x // 2) * 8 + y * 2 + core


class Group:
    def __init__(self, kind):
        x_hi, x_lo, y, z, core = place()
        row, col = lax.axis_index("row"), lax.axis_index("col")
        x = x_hi * 2 + x_lo
        self.size, self.me, self.at = {
            "row": (16, row, lambda i: (i, col)),
            "col": (16, col, lambda i: (row, i)),
            "x": (4, x, lambda i: device(i, y, z, core)),
            "y": (4, y, lambda i: device(x, i, z, core)),
            "z": (8, z, lambda i: device(x, y, i, core)),
            "core": (2, core, lambda i: device(x, y, z, i)),
        }[kind]

    def after(self, step):
        return lax.rem(self.me + step, self.size)

    def before(self, step):
        return lax.rem(self.me + self.size - step, self.size)


def greet(groups):
    barrier = pltpu.get_barrier_semaphore()
    for group in groups:
        for step in range(1, group.size):
            pl.semaphore_signal(barrier, inc=1, device_id=group.at(group.after(step)), device_id_type=MESH)
    pl.semaphore_wait(barrier, sum(group.size - 1 for group in groups))


def send_all(group, source, target, send_sem, recv_sem):
    copies = []
    for step in range(1, group.size):
        to = group.after(step)
        out = pltpu.make_async_remote_copy(
            src_ref=source(to), dst_ref=target(group.me, step), send_sem=send_sem(step), recv_sem=recv_sem(step),
            device_id=group.at(to), device_id_type=MESH)
        out.start()
        back = pltpu.make_async_remote_copy(
            src_ref=source(to), dst_ref=target(group.before(step), step), send_sem=send_sem(step),
            recv_sem=recv_sem(step), device_id=group.at(to), device_id_type=MESH)
        copies.append((out, back))
    return copies


def arrived(copies):
    for _, back in copies:
        back.wait_recv()


def sent(copies):
    for out, _ in copies:
        out.wait_send()


def exchange_start(group, mode, source, target, send_sems, recv_sems, own_sem):
    pick = (lambda i: source.at[i]) if mode == "each" else (lambda i: source)
    own = pltpu.make_async_copy(pick(group.me), target.at[group.me], own_sem)
    own.start()
    copies = send_all(group, pick, lambda i, step: target.at[i], lambda s: send_sems.at[s - 1], lambda s: recv_sems.at[s - 1])
    return own, copies


def exchange_wait(handle):
    own, copies = handle
    own.wait()
    arrived(copies)
    sent(copies)


def exchange_kernel(plan, *refs):
    count = len(plan)
    sources, targets = refs[:count], refs[count:2 * count]
    send_sems, recv_sems, own_sems = refs[2 * count:]
    groups = {kind: Group(kind) for kind, _ in plan}
    greet(list(groups.values()))
    handles = [
        exchange_start(groups[kind], mode, sources[i], targets[i], send_sems.at[i], recv_sems.at[i], own_sems.at[i])
        for i, (kind, mode) in enumerate(plan)
    ]
    for handle in handles:
        exchange_wait(handle)


def exchange(arrays, plan, collective_id):
    shapes = [a.shape if mode == "each" else (16, *a.shape) for a, (_, mode) in zip(arrays, plan)]
    return pl.pallas_call(
        functools.partial(exchange_kernel, tuple(plan)),
        out_shape=[jax.ShapeDtypeStruct(s, a.dtype) for s, a in zip(shapes, arrays)],
        in_specs=[ANY] * len(arrays),
        out_specs=[ANY] * len(arrays),
        scratch_shapes=[DMA((len(arrays), 15)), DMA((len(arrays), 15)), DMA((len(arrays),))],
        compiler_params=pltpu.CompilerParams(collective_id=collective_id, has_side_effects=True),
    )(*arrays)


F32 = jnp.float32
NT = (((1,), (1,)), ((), ()))
LIMIT = 32000.0
DOTS = dict(preferred_element_type=jnp.float32)


def code(pieces, slot):
    top = None
    for piece in pieces:
        size = jnp.abs(piece())
        top = size if top is None else jnp.maximum(top, size)
    top = jnp.max(top, axis=0, keepdims=True)
    level = jnp.ceil(jnp.log2(jnp.maximum(top, 1e-30)) * 16.0)
    row = jnp.broadcast_to(level, (16, 128))
    factor = LIMIT * jnp.exp2(row[0:1] * (-1.0 / 16.0))
    at = 0
    for piece in pieces:
        value = jnp.round(piece() * factor)
        rows = value.shape[0]
        slot[at:at + rows, :] = value.astype(jnp.int32).astype(jnp.int16)
        at += rows
    slot[at:at + 16, :] = row.astype(jnp.int32).astype(jnp.int16)


def wide(value):
    return value.astype(jnp.int32).astype(jnp.float32)


def scale_of(slot, rows):
    return jnp.exp2(wide(slot[rows:rows + 16, :])[0:1] * (1.0 / 16.0)) * (1.0 / LIMIT)


def decode(slot, rows):
    return wide(slot[0:rows, :]) * scale_of(slot, rows)


def squares_of(rows):
    value = rows.astype(F32)
    return jnp.sum(value * value, axis=1, keepdims=True)


def halves(value):
    high = value.astype(jnp.bfloat16)
    return high, (value - high.astype(F32)).astype(jnp.bfloat16)


def main_kernel(owner, chunk, points, squares_row, weights, inverse, wanted, out,
                full, tile, mine, theirs, core_in, x_out, x_in, y_out, y_in, u, v, y_out_2, y_in_2, x_out_2, x_in_2, z_sum,
                z_out, z_in, inverse_in, inverse_all, wanted_in, res_all, delta_all, last_all, res, delta, near_high, near_low,
                send_sems, recv_sems, own_sems):
    x_hi, x_lo, y, z, core = place()
    x = x_hi * 2 + x_lo
    kinds = {kind: Group(kind) for kind in ("row", "col", "x", "y", "z", "core")}
    gx, gy, gz, gc = (kinds[k] for k in ("x", "y", "z", "core"))
    greet([kinds["row"], kinds["col"], gx])
    next_sem = [0]
    started = []

    def send(group, source, target):
        base = next_sem[0]
        next_sem[0] += group.size - 1
        copies = send_all(group, source, target, lambda s: send_sems.at[base + s - 1], lambda s: recv_sems.at[base + s - 1])
        started.append(copies)
        return copies

    def piece(i):
        quarter, lanes = i // 2, i % 2
        return full.at[x_lo, x_hi, y, core, quarter // 2, pl.ds(pl.multiple_of((quarter % 2) * 16, 16), 16),
                       pl.ds(pl.multiple_of(lanes * 512, 512), 512)]

    own_chunk = pltpu.make_async_copy(chunk, piece(z), own_sems.at[0])
    own_chunk.start()
    along_z = send(gz, lambda i: chunk, lambda i, s: piece(i))
    own_inverse = pltpu.make_async_copy(inverse.at[kinds["row"].me], inverse_in.at[kinds["row"].me], own_sems.at[1])
    own_inverse.start()
    own_wanted = pltpu.make_async_copy(wanted.at[kinds["row"].me], wanted_in.at[kinds["row"].me], own_sems.at[2])
    own_wanted.start()
    own_chunk.wait()
    arrived(along_z)
    x_first = send(gx, lambda i: full.at[x_lo, x_hi, y, core, 0], lambda i, s: full.at[i % 2, i // 2, y, core, 0])
    y_first = send(gy, lambda i: full.at[x_lo, x_hi, y, core, 1], lambda i, s: full.at[x_lo, x_hi, i, core, 1])
    arrived(x_first)
    y_last = send(gy, lambda i: full.at[:, :, y, core, 0], lambda i, s: full.at[:, :, i, core, 0])
    arrived(y_first)
    x_last = send(gx, lambda i: full.at[x_lo, x_hi, :, core, 1], lambda i, s: full.at[i % 2, i // 2, :, core, 1])
    inverse_sent = send(kinds["row"], lambda i: inverse.at[i], lambda i, s: inverse_in.at[i])
    wanted_sent = send(kinds["row"], lambda i: wanted.at[i], lambda i, s: wanted_in.at[i])
    arrived(y_last)
    across_0 = send(gc, lambda i: full.at[:, :, :, core, 0], lambda i, s: full.at[:, :, :, i, 0])
    arrived(x_last)
    across_1 = send(gc, lambda i: full.at[:, :, :, core, 1], lambda i, s: full.at[:, :, :, i, 1])

    def products(for_core, hi, pair, target):
        rows = jnp.concatenate([
            full[block, hi, pair * 2 + t, for_core].reshape(64, 1024) for t in range(2) for block in range(2)
        ], axis=0)
        inner = lax.dot_general(rows, points[...], NT, **DOTS)
        distance = squares_of(rows) + squares_row[0:1, :] - 2.0 * inner
        high, low = halves(jnp.exp(-distance * (0.5 / 1024)))
        tile[:, 0:384] = high
        tile[:, 384:768] = high
        tile[:, 768:1152] = low
        for part in range(2):
            span = slice(part * 512, part * 512 + 512)
            result = lax.dot_general(weights[span, :], tile[...], NT, **DOTS)
            target[hi, pair * 2, span, :] = result[:, 0:128]
            target[hi, pair * 2 + 1, span, :] = result[:, 128:256]

    def own_tile(i, carry):
        products(core, i // 2, i % 2, mine)
        return carry

    lax.fori_loop(0, 4, own_tile, 0)
    arrived(across_0)
    arrived(across_1)
    crossing_base = next_sem[0]
    next_sem[0] += 4
    other = (gc.at(gc.after(1)))

    def crossing(i):
        span = pl.ds(pl.multiple_of((i % 2) * 2, 2), 2)
        return pltpu.make_async_remote_copy(
            src_ref=theirs.at[i // 2, span], dst_ref=core_in.at[i // 2, span], send_sem=send_sems.at[crossing_base + i],
            recv_sem=recv_sems.at[crossing_base + i], device_id=other, device_id_type=MESH)

    def other_tile(i, carry):
        products(1 - core, i // 2, i % 2, theirs)
        crossing(i).start()
        return carry

    lax.fori_loop(0, 4, other_tile, 0)

    own_inverse.wait()
    arrived(inverse_sent)
    my_owner = jnp.where(x_lo == 0, owner[0], owner[1])
    inverse_all[kinds["row"].me] = inverse_in[my_owner]
    inverse_spread = send(kinds["row"], lambda i: inverse_all.at[kinds["row"].me], lambda i, s: inverse_all.at[i])

    def join(i, carry):
        crossing(i).wait_recv()
        for t in range(2):
            at = (i // 2, (i % 2) * 2 + t)
            mine[at] += core_in[at]
        return carry

    lax.fori_loop(0, 4, join, 0)

    def part(to_x, to_y, half):
        start = pl.multiple_of(((to_x % 2) * 2 + half) * 256, 256)
        return lambda: mine[to_x // 2, to_y, pl.ds(start, 256), :]

    for step in range(1, 4):
        code([part(gx.after(step), t, 0) for t in range(4)], x_out.at[step - 1])
    x_first = send(gx, lambda i: x_out.at[lax.rem(i + 3 - x, 4)], lambda i, s: x_in.at[s - 1])
    for step in range(1, 4):
        code([part(t, gy.after(step), 1) for t in range(4)], y_out.at[step - 1])
    y_first = send(gy, lambda i: y_out.at[lax.rem(i + 3 - y, 4)], lambda i, s: y_in.at[s - 1])

    first = full[0].reshape(1024, 1024)
    lengths = [
        jnp.transpose(jnp.broadcast_to(squares_of(full[0, t // 4, t % 4].reshape(128, 1024)), (128, 128)))[0:1, :]
        for t in range(8)
    ]
    lengths = jnp.concatenate(lengths, axis=1)
    for t in range(4):
        rows = full[1, t // 2, (t % 2) * 2:(t % 2) * 2 + 2].reshape(256, 1024)
        inner = lax.dot_general(rows, first, NT, **DOTS)
        high, low = halves(jnp.exp(-(squares_of(rows) + lengths - 2.0 * inner) * (0.5 / 1024)))
        near_high[t * 256:t * 256 + 256, :] = high
        near_low[t * 256:t * 256 + 256, :] = low

    arrived(x_first)
    for t in range(4):
        value = part(x, t, 0)()
        for i in range(3):
            value += wide(x_in[i, t * 256:t * 256 + 256, :]) * scale_of(x_in.at[i], 1024)
        u[t] = value
    for step in range(1, 4):
        code([lambda: u[gy.after(step)]], y_out_2.at[step - 1])
    y_last = send(gy, lambda i: y_out_2.at[lax.rem(i + 3 - y, 4)], lambda i, s: y_in_2.at[s - 1])
    arrived(y_first)
    for t in range(4):
        value = part(t, y, 1)()
        for i in range(3):
            value += wide(y_in[i, t * 256:t * 256 + 256, :]) * scale_of(y_in.at[i], 1024)
        v[t] = value
    for step in range(1, 4):
        code([lambda: v[gx.after(step)]], x_out_2.at[step - 1])
    x_last = send(gx, lambda i: x_out_2.at[lax.rem(i + 3 - x, 4)], lambda i, s: x_in_2.at[s - 1])
    arrived(y_last)
    value = u[y]
    for i in range(3):
        value += decode(y_in_2.at[i], 256)
    z_sum[0:256, :] = value
    arrived(x_last)
    value = v[x]
    for i in range(3):
        value += decode(x_in_2.at[i], 256)
    z_sum[256:512, :] = value

    def slab(i):
        return z_sum[pl.ds(pl.multiple_of(i * 64, 64), 64), :]

    for step in range(1, 8):
        code([lambda: slab(gz.after(step))], z_out.at[step - 1])
    to_z = send(gz, lambda i: z_out.at[lax.rem(i + 7 - z, 8)], lambda i, s: z_in.at[s - 1])
    own_wanted.wait()
    arrived(wanted_sent)
    left = lax.broadcasted_iota(jnp.int32, (64, 128), 1) < 64
    goal = jnp.where(left, wanted_in[owner[0]], wanted_in[owner[1]])
    arrived(to_z)
    value = slab(z)
    for i in range(7):
        value += decode(z_in.at[i], 64)
    residual = goal - value

    def spread(group, slots, value):
        code([lambda: value], slots.at[group.me])
        return send(group, lambda i: slots.at[group.me], lambda i, s: slots.at[i])

    def flip(value):
        return pltpu.roll(value, 64, 1)

    copies = spread(kinds["col"], res_all, residual)
    arrived(inverse_spread)
    rows_here = inverse_all[...].reshape(128, 1024)
    arrived(copies)
    for t in range(8):
        even, odd = decode(res_all.at[2 * t], 64), decode(res_all.at[2 * t + 1], 64)
        res[0, :, t * 128:t * 128 + 128] = jnp.where(left, even, flip(odd))
        res[1, :, t * 128:t * 128 + 128] = jnp.where(left, flip(even), odd)
    change_1 = lax.dot_general(res[0], rows_here, NT, precision=lax.Precision.HIGHEST, **DOTS)
    copies = spread(kinds["col"], delta_all, change_1)
    arrived(copies)
    for t in range(8):
        even, odd = decode(delta_all.at[2 * t], 64), decode(delta_all.at[2 * t + 1], 64)
        delta[:, t * 128:t * 128 + 128] = jnp.where(left, even, flip(odd))
    high, low = halves(delta[...])
    both = lax.dot_general(jnp.concatenate([high, low], axis=0), near_high[...], NT, **DOTS)
    moved = both[0:64] + both[64:128] + lax.dot_general(high, near_low[...], NT, **DOTS)
    change_2 = lax.dot_general(res[1] - moved, rows_here, NT, precision=lax.Precision.HIGHEST, **DOTS)
    copies = spread(kinds["row"], last_all, jnp.where(left, change_1, change_2))
    arrived(copies)
    for t in range(8):
        value = jnp.concatenate([decode(last_all.at[2 * t], 64), decode(last_all.at[2 * t + 1], 64)], axis=0)
        out[:, t * 128:t * 128 + 128] = jnp.transpose(value)
    for copies in started:
        sent(copies)

    def leave(i, carry):
        crossing(i).wait_send()
        return carry

    lax.fori_loop(0, 4, leave, 0)


def main(owner, chunk, points, squares_row, weights, inverse, wanted, collective_id):
    i16, bf16 = jnp.int16, jnp.bfloat16
    return pl.pallas_call(
        main_kernel,
        out_shape=jax.ShapeDtypeStruct((128, 1024), F32),
        in_specs=[pl.BlockSpec(memory_space=pltpu.SMEM), VMEM, VMEM, VMEM, VMEM, ANY, ANY],
        out_specs=VMEM,
        scratch_shapes=[
            pltpu.VMEM((2, 2, 4, 2, 2, 32, 1024), bf16),
            pltpu.VMEM((256, 1152), bf16),
            pltpu.VMEM((2, 4, 1024, 128), F32),
            pltpu.VMEM((2, 4, 1024, 128), F32),
            pltpu.VMEM((2, 4, 1024, 128), F32),
            pltpu.VMEM((3, 1040, 128), i16),
            pltpu.VMEM((3, 1040, 128), i16),
            pltpu.VMEM((3, 1040, 128), i16),
            pltpu.VMEM((3, 1040, 128), i16),
            pltpu.VMEM((4, 256, 128), F32),
            pltpu.VMEM((4, 256, 128), F32),
            pltpu.VMEM((3, 272, 128), i16),
            pltpu.VMEM((3, 272, 128), i16),
            pltpu.VMEM((3, 272, 128), i16),
            pltpu.VMEM((3, 272, 128), i16),
            pltpu.VMEM((512, 128), F32),
            pltpu.VMEM((7, 80, 128), i16),
            pltpu.VMEM((7, 80, 128), i16),
            pltpu.VMEM((16, 8, 1024), F32),
            pltpu.VMEM((16, 8, 1024), F32),
            pltpu.VMEM((16, 64, 128), F32),
            pltpu.VMEM((16, 80, 128), i16),
            pltpu.VMEM((16, 80, 128), i16),
            pltpu.VMEM((16, 80, 128), i16),
            pltpu.VMEM((2, 64, 1024), F32),
            pltpu.VMEM((64, 1024), F32),
            pltpu.VMEM((1024, 1024), bf16),
            pltpu.VMEM((1024, 1024), bf16),
            DMA((144,)), DMA((144,)), DMA((3,)),
        ],
        compiler_params=pltpu.CompilerParams(collective_id=collective_id, has_side_effects=True, vmem_limit_bytes=56 * 2**20),
    )(owner, chunk, points, squares_row, weights, inverse, wanted)


def on_device(points, targets, coeffs, block_inverse, block_order):
    blocks_here, per_col, features = points.shape
    classes = targets.shape[2]
    my_row = lax.axis_index("row")
    x_lo = my_row // 8
    ids = [block_order[0], block_order[1]]
    local = [b % blocks_here for b in ids]
    owner = [b // blocks_here for b in ids]

    def pick(array, step):
        return lax.dynamic_index_in_dim(array, local[step], 0, keepdims=False)

    def both(array):
        return jnp.stack([pick(array, 0), pick(array, 1)])

    own_points = both(points).reshape(2, 4, 16, 2, 512).transpose(0, 1, 3, 2, 4).reshape(16, 16, 512)
    (offers,) = exchange([own_points], [("row", "each")], 0)
    my_owner = jnp.where(x_lo == 0, owner[0], owner[1])
    chunk = lax.dynamic_index_in_dim(offers, my_owner, 0, keepdims=False)
    inverse_offer = both(block_inverse).reshape(16, 8, 1024)
    need = both(targets).astype(F32) - ridge_weight * both(coeffs)
    need = jnp.pad(need, ((0, 0), (0, 0), (0, 1024 - classes)))
    wanted_offer = need.transpose(2, 0, 1).reshape(16, 64, 128)

    flat_points = points.reshape(blocks_here * per_col, features)
    flat_wide = flat_points.astype(F32)
    squares_row = jnp.broadcast_to(jnp.sum(flat_wide * flat_wide, axis=1)[None, :], (8, blocks_here * per_col))
    flat_coeffs = jnp.pad(coeffs.reshape(blocks_here * per_col, classes), ((0, 0), (0, 1024 - classes)))
    turned = flat_coeffs.T
    kept = lax.reduce_precision(turned, 8, 7)
    high, low = kept.astype(jnp.bfloat16), (turned - kept).astype(jnp.bfloat16)
    weights = jnp.concatenate([high, low, high], axis=1)
    deltas = main(jnp.stack(owner), chunk, flat_points, squares_row, weights, inverse_offer, wanted_offer, 1)
    deltas = deltas.reshape(2, 64, 1024)[:, :, :classes]

    current = coeffs
    for step in range(2):
        before = lax.dynamic_index_in_dim(current, local[step], 0, keepdims=False)
        updated = jnp.where(my_row == owner[step], before + deltas[step], before)
        current = lax.dynamic_update_index_in_dim(current, updated, local[step], 0)
    return current


def solution(mesh):
    placed = (
        P("row", "col", None),
        P("row", "col", None),
        P("row", "col", None),
        P("row", "col", None),
        P(),
    )
    return jax.shard_map(
        on_device, mesh=mesh, in_specs=placed, out_specs=P("row", "col", None), check_vma=False
    )
```

```python
import functools

import jax
import jax.numpy as jnp
from jax import lax
from jax.experimental import pallas as pl
from jax.experimental.pallas import tpu as pltpu
from jax.sharding import PartitionSpec as P

MESH = pl.DeviceIdType.MESH
ANY = pl.BlockSpec(memory_space=pl.ANY)
VMEM = pl.BlockSpec(memory_space=pltpu.VMEM)
DMA = pltpu.SemaphoreType.DMA

ridge_weight = 1.0


def place():
    row, col = lax.axis_index("row"), lax.axis_index("col")
    return col // 8, row // 8, (col // 2) % 4, row % 8, col % 2


def device(x, y, z, core):
    return (x % 2) * 8 + z, (x // 2) * 8 + y * 2 + core


class Group:
    def __init__(self, kind):
        x_hi, x_lo, y, z, core = place()
        row, col = lax.axis_index("row"), lax.axis_index("col")
        x = x_hi * 2 + x_lo
        self.size, self.me, self.at = {
            "row": (16, row, lambda i: (i, col)),
            "col": (16, col, lambda i: (row, i)),
            "x": (4, x, lambda i: device(i, y, z, core)),
            "y": (4, y, lambda i: device(x, i, z, core)),
            "z": (8, z, lambda i: device(x, y, i, core)),
            "core": (2, core, lambda i: device(x, y, z, i)),
        }[kind]

    def after(self, step):
        return lax.rem(self.me + step, self.size)

    def before(self, step):
        return lax.rem(self.me + self.size - step, self.size)


def greet(groups):
    barrier = pltpu.get_barrier_semaphore()
    for group in groups:
        for step in range(1, group.size):
            pl.semaphore_signal(barrier, inc=1, device_id=group.at(group.after(step)), device_id_type=MESH)
    pl.semaphore_wait(barrier, sum(group.size - 1 for group in groups))


def send_all(group, source, target, send_sem, recv_sem):
    copies = []
    for step in range(1, group.size):
        to = group.after(step)
        out = pltpu.make_async_remote_copy(
            src_ref=source(to), dst_ref=target(group.me, step), send_sem=send_sem(step), recv_sem=recv_sem(step),
            device_id=group.at(to), device_id_type=MESH)
        out.start()
        back = pltpu.make_async_remote_copy(
            src_ref=source(to), dst_ref=target(group.before(step), step), send_sem=send_sem(step),
            recv_sem=recv_sem(step), device_id=group.at(to), device_id_type=MESH)
        copies.append((out, back))
    return copies


def arrived(copies):
    for _, back in copies:
        back.wait_recv()


def sent(copies):
    for out, _ in copies:
        out.wait_send()


F32 = jnp.float32
NT = (((1,), (1,)), ((), ()))
LIMIT = 32000.0
DOTS = dict(preferred_element_type=jnp.float32)


def code(pieces, slot):
    top = None
    for piece in pieces:
        size = jnp.abs(piece())
        top = size if top is None else jnp.maximum(top, size)
    top = jnp.max(top, axis=0, keepdims=True)
    level = jnp.ceil(jnp.log2(jnp.maximum(top, 1e-30)) * 16.0)
    row = jnp.broadcast_to(level, (16, 128))
    factor = LIMIT * jnp.exp2(row[0:1] * (-1.0 / 16.0))
    at = 0
    for piece in pieces:
        value = jnp.round(piece() * factor)
        rows = value.shape[0]
        slot[at:at + rows, :] = value.astype(jnp.int32).astype(jnp.int16)
        at += rows
    slot[at:at + 16, :] = row.astype(jnp.int32).astype(jnp.int16)


def wide(value):
    return value.astype(jnp.int32).astype(jnp.float32)


def scale_of(slot, rows):
    return jnp.exp2(wide(slot[rows:rows + 16, :])[0:1] * (1.0 / 16.0)) * (1.0 / LIMIT)


def decode(slot, rows):
    return wide(slot[0:rows, :]) * scale_of(slot, rows)


def squares_of(rows):
    value = rows.astype(F32)
    return jnp.sum(value * value, axis=1, keepdims=True)


def halves(value):
    high = value.astype(jnp.bfloat16)
    return high, (value - high.astype(F32)).astype(jnp.bfloat16)


def turn(block):
    return jnp.transpose(block)


def main_kernel(owner, offers, points, coeffs, inverse, need, out,
                offers_in, chunk, full, weights, squares_row, tile, mine, theirs, core_in, x_out, x_in, y_out, y_in, u, v,
                y_out_2, y_in_2, x_out_2, x_in_2, z_sum, z_out, z_in, inverse_in, inverse_all, wanted, wanted_in, res_all,
                delta_all, last_all, res, delta, near_high, near_low, send_sems, recv_sems, own_sems):
    x_hi, x_lo, y, z, core = place()
    x = x_hi * 2 + x_lo
    kinds = {kind: Group(kind) for kind in ("row", "col", "x", "y", "z", "core")}
    gx, gy, gz, gc, gr = (kinds[k] for k in ("x", "y", "z", "core", "row"))
    greet([gr, kinds["col"], gx])
    next_sem = [0]
    started = []

    def take(count):
        next_sem[0] += count
        return next_sem[0] - count

    def send(group, source, target):
        base = take(group.size - 1)
        copies = send_all(group, source, target, lambda s: send_sems.at[base + s - 1], lambda s: recv_sems.at[base + s - 1])
        started.append(copies)
        return copies

    own_offer = pltpu.make_async_copy(offers.at[gr.me], offers_in.at[gr.me], own_sems.at[0])
    own_offer.start()
    offered = send(gr, lambda i: offers.at[i], lambda i, s: offers_in.at[i])
    for a in range(3):
        span = slice(a * 128, a * 128 + 128)
        squares_row[:, span] = turn(jnp.broadcast_to(squares_of(points[span, :]), (128, 128)))[0:8]
        for b in range(8):
            high, low = halves(turn(coeffs[span, b * 128:b * 128 + 128]))
            weights[b * 128:b * 128 + 128, a * 128:a * 128 + 128] = high
            weights[b * 128:b * 128 + 128, a * 128 + 384:a * 128 + 512] = low
            weights[b * 128:b * 128 + 128, a * 128 + 768:a * 128 + 896] = high
    for b in range(8):
        block = turn(need[:, :, b * 128:b * 128 + 128].reshape(128, 128))
        wanted[2 * b] = block[0:64]
        wanted[2 * b + 1] = block[64:128]
    own_offer.wait()
    arrived(offered)
    my_owner = jnp.where(x_lo == 0, owner[0], owner[1])
    chunk[...] = offers_in[my_owner]

    def piece(i):
        quarter, lanes = i // 2, i % 2
        return full.at[x_lo, x_hi, y, core, quarter // 2, pl.ds(pl.multiple_of((quarter % 2) * 16, 16), 16),
                       pl.ds(pl.multiple_of(lanes * 512, 512), 512)]

    own_chunk = pltpu.make_async_copy(chunk, piece(z), own_sems.at[3])
    own_chunk.start()
    along_z = send(gz, lambda i: chunk, lambda i, s: piece(i))
    own_chunk.wait()
    arrived(along_z)
    x_first = send(gx, lambda i: full.at[x_lo, x_hi, y, core, 0], lambda i, s: full.at[i % 2, i // 2, y, core, 0])
    y_first = send(gy, lambda i: full.at[x_lo, x_hi, y, core, 1], lambda i, s: full.at[x_lo, x_hi, i, core, 1])
    arrived(x_first)
    y_last = send(gy, lambda i: full.at[:, :, y, core, 0], lambda i, s: full.at[:, :, i, core, 0])
    arrived(y_first)
    x_last = send(gx, lambda i: full.at[x_lo, x_hi, :, core, 1], lambda i, s: full.at[i % 2, i // 2, :, core, 1])
    arrived(y_last)
    across_0 = send(gc, lambda i: full.at[:, :, :, core, 0], lambda i, s: full.at[:, :, :, i, 0])
    arrived(x_last)
    across_1 = send(gc, lambda i: full.at[:, :, :, core, 1], lambda i, s: full.at[:, :, :, i, 1])

    own_inverse = pltpu.make_async_copy(inverse.at[gr.me], inverse_in.at[gr.me], own_sems.at[1])
    own_inverse.start()
    own_wanted = pltpu.make_async_copy(wanted.at[gr.me], wanted_in.at[gr.me], own_sems.at[2])
    own_wanted.start()
    inverse_sent = send(gr, lambda i: inverse.at[i], lambda i, s: inverse_in.at[i])
    wanted_sent = send(gr, lambda i: wanted.at[i], lambda i, s: wanted_in.at[i])

    def near(for_core, i):
        rows = jnp.concatenate([
            full[block, i // 2, (i % 2) * 2 + t, for_core].reshape(64, 1024) for t in range(2) for block in range(2)
        ], axis=0)
        inner = lax.dot_general(rows, points[...], NT, **DOTS)
        distance = squares_of(rows) + squares_row[0:1, :] - 2.0 * inner
        high, low = halves(jnp.exp(-distance * (0.5 / 1024)))
        tile[for_core, i, :, 0:384] = high
        tile[for_core, i, :, 384:768] = high
        tile[for_core, i, :, 768:1152] = low

    def own_tile(i, carry):
        near(core, i)
        return carry

    def other_tile(i, carry):
        near(1 - core, i)
        return carry

    lax.fori_loop(0, 4, own_tile, 0)
    arrived(across_0)
    arrived(across_1)
    lax.fori_loop(0, 4, other_tile, 0)

    crossing_base = take(4)
    x_base, y_base = take(3), take(6)

    def crossing(quarter):
        return pltpu.make_async_remote_copy(
            src_ref=theirs.at[quarter], dst_ref=core_in.at[quarter], send_sem=send_sems.at[crossing_base + quarter],
            recv_sem=recv_sems.at[crossing_base + quarter], device_id=gc.at(gc.after(1)), device_id_type=MESH)

    def products(for_core, quarter, target):
        part = weights[quarter * 256:quarter * 256 + 256, :]
        result = lax.dot_general(part, tile[for_core].reshape(1024, 1152), NT, **DOTS)
        for i in range(8):
            target[quarter, i // 4, i % 4] = result[:, i * 128:i * 128 + 128]

    def summed(quarter, to_hi, to_y):
        return lambda: mine[quarter, to_hi, to_y] + core_in[quarter, to_hi, to_y]

    def x_copy(to, slot):
        return pltpu.make_async_remote_copy(
            src_ref=x_out.at[slot], dst_ref=x_in.at[slot], send_sem=send_sems.at[x_base + slot],
            recv_sem=recv_sems.at[x_base + slot], device_id=gx.at(to), device_id_type=MESH)

    def y_copy(step, low):
        return pltpu.make_async_remote_copy(
            src_ref=y_out.at[step - 1, low], dst_ref=y_in.at[step - 1, low],
            send_sem=send_sems.at[y_base + 2 * (step - 1) + low], recv_sem=recv_sems.at[y_base + 2 * (step - 1) + low],
            device_id=gy.at(gy.after(step)), device_id_type=MESH)

    def leave_quarter(quarter):
        low, half = quarter // 2, quarter % 2
        crossing(quarter).wait_recv()
        if half == 0:
            for high in range(2):
                to = high * 2 + low

                @pl.when(to != x)
                def _(high=high, to=to):
                    slot = lax.rem(to + 3 - x, 4)
                    code([summed(quarter, high, t) for t in range(4)], x_out.at[slot])
                    x_copy(to, slot).start()
        else:
            for step in range(1, 4):
                code([summed(quarter, t, gy.after(step)) for t in range(2)], y_out.at[step - 1, low])
                y_copy(step, low).start()

    order = (0, 1, 2, 3)
    for place_in, quarter in enumerate(order):
        products(1 - core, quarter, theirs)
        crossing(quarter).start()
        products(core, quarter, mine)
        if place_in:
            leave_quarter(order[place_in - 1])
    leave_quarter(order[3])

    own_inverse.wait()
    arrived(inverse_sent)
    inverse_all[gr.me] = inverse_in[my_owner]
    inverse_spread = send(gr, lambda i: inverse_all.at[gr.me], lambda i, s: inverse_all.at[i])

    first = full[0].reshape(1024, 1024)
    lengths = [
        jnp.transpose(jnp.broadcast_to(squares_of(full[0, t // 4, t % 4].reshape(128, 1024)), (128, 128)))[0:1, :]
        for t in range(8)
    ]
    lengths = jnp.concatenate(lengths, axis=1)
    for t in range(4):
        rows = full[1, t // 2, (t % 2) * 2:(t % 2) * 2 + 2].reshape(256, 1024)
        inner = lax.dot_general(rows, first, NT, **DOTS)
        high, low = halves(jnp.exp(-(squares_of(rows) + lengths - 2.0 * inner) * (0.5 / 1024)))
        near_high[t * 256:t * 256 + 256, :] = high
        near_low[t * 256:t * 256 + 256, :] = low

    for slot in range(3):
        x_copy(gx.after(slot + 1), slot).wait_recv()
    for t in range(4):
        value = summed(2 * x_lo, x_hi, t)()
        for i in range(3):
            value += wide(x_in[i, t * 256:t * 256 + 256, :]) * scale_of(x_in.at[i], 1024)
        u[t] = value
    for step in range(1, 4):
        code([lambda: u[gy.after(step)]], y_out_2.at[step - 1])
    y_last = send(gy, lambda i: y_out_2.at[lax.rem(i + 3 - y, 4)], lambda i, s: y_in_2.at[s - 1])
    for step in range(1, 4):
        for low in range(2):
            y_copy(step, low).wait_recv()
    for t in range(4):
        value = summed(2 * (t % 2) + 1, t // 2, y)()
        for i in range(3):
            slot = y_in.at[i, t % 2]
            value += wide(y_in[i, t % 2, (t // 2) * 256:(t // 2) * 256 + 256, :]) * scale_of(slot, 512)
        v[t] = value
    for step in range(1, 4):
        code([lambda: v[gx.after(step)]], x_out_2.at[step - 1])
    x_last = send(gx, lambda i: x_out_2.at[lax.rem(i + 3 - x, 4)], lambda i, s: x_in_2.at[s - 1])
    arrived(y_last)
    value = u[y]
    for i in range(3):
        value += decode(y_in_2.at[i], 256)
    z_sum[0:256, :] = value
    arrived(x_last)
    value = v[x]
    for i in range(3):
        value += decode(x_in_2.at[i], 256)
    z_sum[256:512, :] = value

    def slab(i):
        return z_sum[pl.ds(pl.multiple_of(i * 64, 64), 64), :]

    for step in range(1, 8):
        code([lambda: slab(gz.after(step))], z_out.at[step - 1])
    to_z = send(gz, lambda i: z_out.at[lax.rem(i + 7 - z, 8)], lambda i, s: z_in.at[s - 1])
    own_wanted.wait()
    arrived(wanted_sent)
    left = lax.broadcasted_iota(jnp.int32, (64, 128), 1) < 64
    goal = jnp.where(left, wanted_in[owner[0]], wanted_in[owner[1]])
    arrived(to_z)
    value = slab(z)
    for i in range(7):
        value += decode(z_in.at[i], 64)
    residual = goal - value

    def spread(group, slots, value):
        code([lambda: value], slots.at[group.me])
        return send(group, lambda i: slots.at[group.me], lambda i, s: slots.at[i])

    def flip(value):
        return pltpu.roll(value, 64, 1)

    copies = spread(kinds["col"], res_all, residual)
    arrived(inverse_spread)
    rows_here = inverse_all[...].reshape(128, 1024)
    arrived(copies)
    for t in range(8):
        even, odd = decode(res_all.at[2 * t], 64), decode(res_all.at[2 * t + 1], 64)
        res[0, :, t * 128:t * 128 + 128] = jnp.where(left, even, flip(odd))
        res[1, :, t * 128:t * 128 + 128] = jnp.where(left, flip(even), odd)
    change_1 = lax.dot_general(res[0], rows_here, NT, precision=lax.Precision.HIGHEST, **DOTS)
    copies = spread(kinds["col"], delta_all, change_1)
    arrived(copies)
    for t in range(8):
        even, odd = decode(delta_all.at[2 * t], 64), decode(delta_all.at[2 * t + 1], 64)
        delta[:, t * 128:t * 128 + 128] = jnp.where(left, even, flip(odd))
    high, low = halves(delta[...])
    both = lax.dot_general(jnp.concatenate([high, low], axis=0), near_high[...], NT, **DOTS)
    moved = both[0:64] + both[64:128] + lax.dot_general(high, near_low[...], NT, **DOTS)
    change_2 = lax.dot_general(res[1] - moved, rows_here, NT, precision=lax.Precision.HIGHEST, **DOTS)
    copies = spread(gr, last_all, jnp.where(left, change_1, change_2))
    arrived(copies)
    for t in range(8):
        value = jnp.concatenate([decode(last_all.at[2 * t], 64), decode(last_all.at[2 * t + 1], 64)], axis=0)
        out[:, t * 128:t * 128 + 128] = jnp.transpose(value)
    for copies in started:
        sent(copies)

    for slot in range(3):
        x_copy(gx.after(slot + 1), slot).wait_send()
    for step in range(1, 4):
        for low in range(2):
            y_copy(step, low).wait_send()
    for quarter in range(4):
        crossing(quarter).wait_send()


def main(owner, offers, points, coeffs, inverse, need, collective_id):
    i16, bf16 = jnp.int16, jnp.bfloat16
    return pl.pallas_call(
        main_kernel,
        out_shape=jax.ShapeDtypeStruct((128, 1024), F32),
        in_specs=[pl.BlockSpec(memory_space=pltpu.SMEM), ANY, VMEM, VMEM, ANY, VMEM],
        out_specs=VMEM,
        scratch_shapes=[
            pltpu.VMEM((16, 16, 512), bf16),
            pltpu.VMEM((16, 512), bf16),
            pltpu.VMEM((2, 2, 4, 2, 2, 32, 1024), bf16),
            pltpu.VMEM((1024, 1152), bf16),
            pltpu.VMEM((8, 384), F32),
            pltpu.VMEM((2, 4, 256, 1152), bf16),
            pltpu.VMEM((4, 2, 4, 256, 128), F32),
            pltpu.VMEM((4, 2, 4, 256, 128), F32),
            pltpu.VMEM((4, 2, 4, 256, 128), F32),
            pltpu.VMEM((3, 1040, 128), i16),
            pltpu.VMEM((3, 1040, 128), i16),
            pltpu.VMEM((3, 2, 528, 128), i16),
            pltpu.VMEM((3, 2, 528, 128), i16),
            pltpu.VMEM((4, 256, 128), F32),
            pltpu.VMEM((4, 256, 128), F32),
            pltpu.VMEM((3, 272, 128), i16),
            pltpu.VMEM((3, 272, 128), i16),
            pltpu.VMEM((3, 272, 128), i16),
            pltpu.VMEM((3, 272, 128), i16),
            pltpu.VMEM((512, 128), F32),
            pltpu.VMEM((7, 80, 128), i16),
            pltpu.VMEM((7, 80, 128), i16),
            pltpu.VMEM((16, 8, 1024), F32),
            pltpu.VMEM((16, 8, 1024), F32),
            pltpu.VMEM((16, 64, 128), F32),
            pltpu.VMEM((16, 64, 128), F32),
            pltpu.VMEM((16, 80, 128), i16),
            pltpu.VMEM((16, 80, 128), i16),
            pltpu.VMEM((16, 80, 128), i16),
            pltpu.VMEM((2, 64, 1024), F32),
            pltpu.VMEM((64, 1024), F32),
            pltpu.VMEM((1024, 1024), bf16),
            pltpu.VMEM((1024, 1024), bf16),
            DMA((160,)), DMA((160,)), DMA((4,)),
        ],
        compiler_params=pltpu.CompilerParams(collective_id=collective_id, has_side_effects=True, vmem_limit_bytes=56 * 2**20),
    )(owner, offers, points, coeffs, inverse, need)


def on_device(points, targets, coeffs, block_inverse, block_order):
    blocks_here, per_col, features = points.shape
    classes = targets.shape[2]
    my_row = lax.axis_index("row")
    ids = [block_order[0], block_order[1]]
    local = [b % blocks_here for b in ids]
    owner = [b // blocks_here for b in ids]

    def pick(array, step):
        return lax.dynamic_index_in_dim(array, local[step], 0, keepdims=False)

    def both(array):
        return jnp.stack([pick(array, 0), pick(array, 1)])

    own_points = both(points).reshape(2, 4, 16, 2, 512).transpose(0, 1, 3, 2, 4).reshape(16, 16, 512)
    inverse_offer = both(block_inverse).reshape(16, 8, 1024)
    need = both(targets).astype(F32) - ridge_weight * both(coeffs)
    need = jnp.pad(need, ((0, 0), (0, 0), (0, 1024 - classes)))

    flat_points = points.reshape(blocks_here * per_col, features)
    flat_coeffs = jnp.pad(coeffs.reshape(blocks_here * per_col, classes), ((0, 0), (0, 1024 - classes)))
    deltas = main(jnp.stack(owner), own_points, flat_points, flat_coeffs, inverse_offer, need, 0)
    deltas = deltas.reshape(2, 64, 1024)[:, :, :classes]

    current = coeffs
    for step in range(2):
        before = lax.dynamic_index_in_dim(current, local[step], 0, keepdims=False)
        updated = jnp.where(my_row == owner[step], before + deltas[step], before)
        current = lax.dynamic_update_index_in_dim(current, updated, local[step], 0)
    return current


def solution(mesh):
    placed = (
        P("row", "col", None),
        P("row", "col", None),
        P("row", "col", None),
        P("row", "col", None),
        P(),
    )
    return jax.shard_map(
        on_device, mesh=mesh, in_specs=placed, out_specs=P("row", "col", None), check_vma=False
    )
```

```python
import functools

import jax
import jax.numpy as jnp
from jax import lax
from jax.experimental import pallas as pl
from jax.experimental.pallas import tpu as pltpu
from jax.sharding import PartitionSpec as P

MESH = pl.DeviceIdType.MESH
ANY = pl.BlockSpec(memory_space=pl.ANY)
VMEM = pl.BlockSpec(memory_space=pltpu.VMEM)
DMA = pltpu.SemaphoreType.DMA

ridge_weight = 1.0


def place():
    row, col = lax.axis_index("row"), lax.axis_index("col")
    return col // 8, row // 8, (col // 2) % 4, row % 8, col % 2


def device(x, y, z, core):
    return (x % 2) * 8 + z, (x // 2) * 8 + y * 2 + core


class Group:
    def __init__(self, kind):
        x_hi, x_lo, y, z, core = place()
        row, col = lax.axis_index("row"), lax.axis_index("col")
        x = x_hi * 2 + x_lo
        self.size, self.me, self.at = {
            "row": (16, row, lambda i: (i, col)),
            "col": (16, col, lambda i: (row, i)),
            "x": (4, x, lambda i: device(i, y, z, core)),
            "y": (4, y, lambda i: device(x, i, z, core)),
            "z": (8, z, lambda i: device(x, y, i, core)),
            "core": (2, core, lambda i: device(x, y, z, i)),
        }[kind]

    def after(self, step):
        return lax.rem(self.me + step, self.size)

    def before(self, step):
        return lax.rem(self.me + self.size - step, self.size)


def signal_all(groups):
    barrier = pltpu.get_barrier_semaphore()
    for group in groups:
        for step in range(1, group.size):
            pl.semaphore_signal(barrier, inc=1, device_id=group.at(group.after(step)), device_id_type=MESH)


def wait_all(groups):
    pl.semaphore_wait(pltpu.get_barrier_semaphore(), sum(group.size - 1 for group in groups))


def send_all(group, source, target, send_sem, recv_sem):
    copies = []
    for step in range(1, group.size):
        to = group.after(step)
        out = pltpu.make_async_remote_copy(
            src_ref=source(to), dst_ref=target(group.me, step), send_sem=send_sem(step), recv_sem=recv_sem(step),
            device_id=group.at(to), device_id_type=MESH)
        out.start()
        back = pltpu.make_async_remote_copy(
            src_ref=source(to), dst_ref=target(group.before(step), step), send_sem=send_sem(step),
            recv_sem=recv_sem(step), device_id=group.at(to), device_id_type=MESH)
        copies.append((out, back))
    return copies


def arrived(copies):
    for _, back in copies:
        back.wait_recv()


def sent(copies):
    for out, _ in copies:
        out.wait_send()


F32 = jnp.float32
NT = (((1,), (1,)), ((), ()))
NN = (((1,), (0,)), ((), ()))
LIMIT = 32000.0
DOTS = dict(preferred_element_type=jnp.float32)


def code(pieces, slot):
    top = None
    for piece in pieces:
        size = jnp.abs(piece())
        top = size if top is None else jnp.maximum(top, size)
    top = jnp.max(top, axis=0, keepdims=True)
    level = jnp.ceil(jnp.log2(jnp.maximum(top, 1e-30)) * 16.0)
    row = jnp.broadcast_to(level, (16, 128))
    factor = LIMIT * jnp.exp2(row[0:1] * (-1.0 / 16.0))
    at = 0
    for piece in pieces:
        value = jnp.round(piece() * factor)
        rows = value.shape[0]
        slot[at:at + rows, :] = value.astype(jnp.int32).astype(jnp.int16)
        at += rows
    slot[at:at + 16, :] = row.astype(jnp.int32).astype(jnp.int16)


def wide(value):
    return value.astype(jnp.int32).astype(jnp.float32)


def scale_of(slot, rows):
    return jnp.exp2(wide(slot[rows:rows + 16, :])[0:1] * (1.0 / 16.0)) * (1.0 / LIMIT)


def decode(slot, rows):
    return wide(slot[0:rows, :]) * scale_of(slot, rows)


def squares_of(rows):
    value = rows.astype(F32)
    return jnp.sum(value * value, axis=1, keepdims=True)


def halves(value):
    high = value.astype(jnp.bfloat16)
    return high, (value - high.astype(F32)).astype(jnp.bfloat16)


def turn(block):
    rows, lanes = block.shape
    if lanes < 128:
        block = jnp.concatenate([block, jnp.zeros((rows, 128 - lanes), block.dtype)], axis=1)
    return jnp.transpose(block)


def main_kernel(order, points, targets, coeffs, block_inverse, out,
                offers, inverse, offers_in, chunk, full, weights, squares_row, tile, mine, apart, theirs, core_in, x_out, x_in, y_out, y_in, u, v,
                y_out_2, y_in_2, x_out_2, x_in_2, z_sum, z_out, z_in, inverse_in, inverse_all, wanted, wanted_in, res_all,
                delta_all, last_all, res, delta, near_high, near_low, linked, send_sems, recv_sems, own_sems):
    x_hi, x_lo, y, z, core = place()
    x = x_hi * 2 + x_lo
    classes = coeffs.shape[2]
    blocks_here = points.shape[0]
    owner, local = [order[t] // blocks_here for t in range(2)], [order[t] % blocks_here for t in range(2)]
    kinds = {kind: Group(kind) for kind in ("row", "col", "x", "y", "z", "core")}
    gx, gy, gz, gc, gr = (kinds[k] for k in ("x", "y", "z", "core", "row"))
    signal_all([gr, kinds["col"], gx])
    for block in range(2):
        for q in range(8):
            offers[block * 8 + q] = points[local[block], (q // 2) * 16:(q // 2) * 16 + 16, (q % 2) * 512:(q % 2) * 512 + 512]
    wait_all([gr, kinds["col"], gx])
    next_sem = [0]
    started = []

    def take(count):
        next_sem[0] += count
        return next_sem[0] - count

    def send(group, source, target):
        base = take(group.size - 1)
        copies = send_all(group, source, target, lambda s: send_sems.at[base + s - 1], lambda s: recv_sems.at[base + s - 1])
        started.append(copies)
        return copies

    own_offer = pltpu.make_async_copy(offers.at[gr.me], offers_in.at[gr.me], own_sems.at[0])
    own_offer.start()
    offered = send(gr, lambda i: offers.at[i], lambda i, s: offers_in.at[i])
    for a in range(3):
        span = slice(a * 128, a * 128 + 128)
        squares_row[:, span] = turn(jnp.broadcast_to(squares_of(points[2 * a:2 * a + 2].reshape(128, 1024)), (128, 128)))[0:8]
        for b in range(8):
            high, low = halves(turn(coeffs[2 * a:2 * a + 2, :, b * 128:min(b * 128 + 128, classes)].reshape(128, -1)))
            weights[b * 128:b * 128 + 128, a * 128:a * 128 + 128] = high
            weights[b * 128:b * 128 + 128, a * 128 + 384:a * 128 + 512] = low
            weights[b * 128:b * 128 + 128, a * 128 + 768:a * 128 + 896] = high
    for b in range(8):
        lanes = slice(b * 128, min(b * 128 + 128, classes))
        block = turn(jnp.concatenate([
            targets[local[t], :, lanes].astype(F32) - ridge_weight * coeffs[local[t], :, lanes] for t in range(2)
        ], axis=0))
        code([lambda: block[0:64]], wanted.at[2 * b])
        code([lambda: block[64:128]], wanted.at[2 * b + 1])
    for q in range(16):
        inverse[q] = block_inverse[local[q // 8], (q % 8) * 8:(q % 8) * 8 + 8, :]
    own_offer.wait()
    arrived(offered)
    my_owner = jnp.where(x_lo == 0, owner[0], owner[1])
    chunk[...] = offers_in[my_owner]

    def piece(i):
        quarter, lanes = i // 2, i % 2
        return full.at[x_lo, x_hi, y, core, quarter // 2, pl.ds(pl.multiple_of((quarter % 2) * 16, 16), 16),
                       pl.ds(pl.multiple_of(lanes * 512, 512), 512)]

    own_chunk = pltpu.make_async_copy(chunk, piece(z), own_sems.at[3])
    own_chunk.start()
    along_z = send(gz, lambda i: chunk, lambda i, s: piece(i))
    own_chunk.wait()
    arrived(along_z)
    x_first = send(gx, lambda i: full.at[x_lo, x_hi, y, core, 0], lambda i, s: full.at[i % 2, i // 2, y, core, 0])
    y_first = send(gy, lambda i: full.at[x_lo, x_hi, y, core, 1], lambda i, s: full.at[x_lo, x_hi, i, core, 1])
    arrived(x_first)
    y_last = send(gy, lambda i: full.at[:, :, y, core, 0], lambda i, s: full.at[:, :, i, core, 0])
    arrived(y_first)
    x_last = send(gx, lambda i: full.at[x_lo, x_hi, :, core, 1], lambda i, s: full.at[i % 2, i // 2, :, core, 1])
    own_inverse = pltpu.make_async_copy(inverse.at[gr.me], inverse_in.at[gr.me], own_sems.at[1])
    own_inverse.start()
    inverse_sent = send(gr, lambda i: inverse.at[i], lambda i, s: inverse_in.at[i])
    arrived(y_last)
    across_0 = send(gc, lambda i: full.at[:, :, :, core, 0], lambda i, s: full.at[:, :, :, i, 0])
    arrived(x_last)
    across_1 = send(gc, lambda i: full.at[:, :, :, core, 1], lambda i, s: full.at[:, :, :, i, 1])

    def near(for_core, i):
        rows = jnp.concatenate([
            full[block, i // 2, (i % 2) * 2 + t, for_core].reshape(64, 1024) for t in range(2) for block in range(2)
        ], axis=0)
        inner = lax.dot_general(rows, points[...].reshape(384, 1024), NT, **DOTS)
        distance = squares_of(rows) + squares_row[0:1, :] - 2.0 * inner
        high, low = halves(jnp.exp(-distance * (0.5 / 1024)))
        tile[for_core, i, :, 0:384] = high
        tile[for_core, i, :, 384:768] = high
        tile[for_core, i, :, 768:1152] = low

    def own_tile(i, carry):
        near(core, i)
        return carry

    def other_tile(i, carry):
        near(1 - core, i)
        return carry

    lax.fori_loop(0, 4, own_tile, 0)
    own_inverse.wait()
    arrived(inverse_sent)
    inverse_all[gr.me] = inverse_in[my_owner]
    inverse_spread = send(gr, lambda i: inverse_all.at[gr.me], lambda i, s: inverse_all.at[i])
    wanted_sent = send(gr, lambda i: wanted.at[i], lambda i, s: wanted_in.at[i])
    arrived(across_0)
    arrived(across_1)
    lax.fori_loop(0, 4, other_tile, 0)

    crossing_base = take(4)
    x_base, y_base = take(3), take(6)

    def crossing(quarter):
        return pltpu.make_async_remote_copy(
            src_ref=theirs.at[quarter], dst_ref=core_in.at[quarter], send_sem=send_sems.at[crossing_base + quarter],
            recv_sem=recv_sems.at[crossing_base + quarter], device_id=gc.at(gc.after(1)), device_id_type=MESH)

    def products(for_core, quarter):
        part = weights[quarter * 256:quarter * 256 + 256, :]
        return lax.dot_general(part, tile[for_core].reshape(1024, 1152), NT, **DOTS)

    def summed(quarter, to_hi, to_y):
        return lambda: mine[quarter, to_hi, to_y]

    def x_copy(to, slot):
        return pltpu.make_async_remote_copy(
            src_ref=x_out.at[slot], dst_ref=x_in.at[slot], send_sem=send_sems.at[x_base + slot],
            recv_sem=recv_sems.at[x_base + slot], device_id=gx.at(to), device_id_type=MESH)

    def y_copy(step, low):
        return pltpu.make_async_remote_copy(
            src_ref=y_out.at[step - 1, low], dst_ref=y_in.at[step - 1, low],
            send_sem=send_sems.at[y_base + 2 * (step - 1) + low], recv_sem=recv_sems.at[y_base + 2 * (step - 1) + low],
            device_id=gy.at(gy.after(step)), device_id_type=MESH)

    def leave_quarter(quarter):
        low, half = quarter // 2, quarter % 2
        crossing(quarter).wait_recv()
        factor = scale_of(core_in.at[quarter], 2048)
        for i in range(8):
            mine[quarter, i // 4, i % 4] += wide(core_in[quarter, i * 256:i * 256 + 256, :]) * factor
        if half == 0:
            for high in range(2):
                to = high * 2 + low

                @pl.when(to != x)
                def _(high=high, to=to):
                    slot = lax.rem(to + 3 - x, 4)
                    code([summed(quarter, high, t) for t in range(4)], x_out.at[slot])
                    x_copy(to, slot).start()
        else:
            for step in range(1, 4):
                code([summed(quarter, t, gy.after(step)) for t in range(2)], y_out.at[step - 1, low])
                y_copy(step, low).start()

    for quarter in range(4):
        result = products(1 - core, quarter)
        for i in range(8):
            apart[i] = result[:, i * 128:i * 128 + 128]
        code([lambda i=i: apart[i] for i in range(8)], theirs.at[quarter])
        crossing(quarter).start()
    for quarter in range(4):
        result = products(core, quarter)
        for i in range(8):
            mine[quarter, i // 4, i % 4] = result[:, i * 128:i * 128 + 128]
        leave_quarter(quarter)

    for slot in range(3):
        x_copy(gx.after(slot + 1), slot).wait_recv()
    for t in range(4):
        value = summed(2 * x_lo, x_hi, t)()
        for i in range(3):
            value += wide(x_in[i, t * 256:t * 256 + 256, :]) * scale_of(x_in.at[i], 1024)
        u[t] = value
    for step in range(1, 4):
        code([lambda: u[gy.after(step)]], y_out_2.at[step - 1])
    y_last = send(gy, lambda i: y_out_2.at[lax.rem(i + 3 - y, 4)], lambda i, s: y_in_2.at[s - 1])
    for step in range(1, 4):
        for low in range(2):
            y_copy(step, low).wait_recv()
    for t in range(4):
        value = summed(2 * (t % 2) + 1, t // 2, y)()
        for i in range(3):
            slot = y_in.at[i, t % 2]
            value += wide(y_in[i, t % 2, (t // 2) * 256:(t // 2) * 256 + 256, :]) * scale_of(slot, 512)
        v[t] = value
    for step in range(1, 4):
        code([lambda: v[gx.after(step)]], x_out_2.at[step - 1])
    x_last = send(gx, lambda i: x_out_2.at[lax.rem(i + 3 - x, 4)], lambda i, s: x_in_2.at[s - 1])
    arrived(y_last)
    value = u[y]
    for i in range(3):
        value += decode(y_in_2.at[i], 256)
    z_sum[0:256, :] = value
    arrived(x_last)
    value = v[x]
    for i in range(3):
        value += decode(x_in_2.at[i], 256)
    z_sum[256:512, :] = value

    def slab(i):
        return z_sum[pl.ds(pl.multiple_of(i * 64, 64), 64), :]

    for step in range(1, 8):
        code([lambda: slab(gz.after(step))], z_out.at[step - 1])
    to_z = send(gz, lambda i: z_out.at[lax.rem(i + 7 - z, 8)], lambda i, s: z_in.at[s - 1])
    first = full[0].reshape(1024, 1024)
    lengths = [
        jnp.transpose(jnp.broadcast_to(squares_of(full[0, t // 4, t % 4].reshape(128, 1024)), (128, 128)))[0:1, :]
        for t in range(8)
    ]
    lengths = jnp.concatenate(lengths, axis=1)
    for t in range(4):
        rows = full[1, t // 2, (t % 2) * 2:(t % 2) * 2 + 2].reshape(256, 1024)
        inner = lax.dot_general(rows, first, NT, **DOTS)
        high, low = halves(jnp.exp(-(squares_of(rows) + lengths - 2.0 * inner) * (0.5 / 1024)))
        near_high[t * 256:t * 256 + 256, :] = high
        near_low[t * 256:t * 256 + 256, :] = low

    left = lax.broadcasted_iota(jnp.int32, (64, 128), 1) < 64
    wanted_in[gr.me] = wanted[gr.me]
    arrived(wanted_sent)
    goal = jnp.where(left, decode(wanted_in[owner[0]], 64), decode(wanted_in[owner[1]], 64))
    arrived(to_z)
    value = slab(z)
    for i in range(7):
        value += decode(z_in.at[i], 64)
    residual = goal - value

    def spread(group, slots, value):
        code([lambda: value], slots.at[group.me])
        return send(group, lambda i: slots.at[group.me], lambda i, s: slots.at[i])

    def flip(value):
        return pltpu.roll(value, 64, 1)

    copies = spread(kinds["col"], res_all, residual)
    arrived(inverse_spread)
    rows_here = inverse_all[...].reshape(128, 1024)
    high, low = halves(rows_here)
    across = lax.dot_general(jnp.concatenate([high, low], axis=0), near_high[...], NN, **DOTS)
    linked[...] = across[0:128] + across[128:256] + lax.dot_general(high, near_low[...], NN, **DOTS)
    arrived(copies)
    for t in range(8):
        even, odd = decode(res_all.at[2 * t], 64), decode(res_all.at[2 * t + 1], 64)
        res[0, :, t * 128:t * 128 + 128] = jnp.where(left, even, flip(odd))
        res[1, :, t * 128:t * 128 + 128] = jnp.where(left, flip(even), odd)
    change_1 = lax.dot_general(res[0], rows_here, NT, precision=lax.Precision.HIGHEST, **DOTS)
    copies = spread(kinds["col"], delta_all, change_1)
    change_2 = lax.dot_general(res[1], rows_here, NT, precision=lax.Precision.HIGHEST, **DOTS)
    arrived(copies)
    for t in range(8):
        even, odd = decode(delta_all.at[2 * t], 64), decode(delta_all.at[2 * t + 1], 64)
        delta[:, t * 128:t * 128 + 128] = jnp.where(left, even, flip(odd))
    change_2 -= lax.dot_general(delta[...], linked[...], NT, precision=lax.Precision.HIGHEST, **DOTS)
    copies = spread(gr, last_all, jnp.where(left, change_1, change_2))
    arrived(copies)
    for t in range(8):
        value = jnp.concatenate([decode(last_all.at[2 * t], 64), decode(last_all.at[2 * t + 1], 64)], axis=0)
        lanes = min(128, classes - t * 128)
        out[:, t * 128:t * 128 + lanes] = jnp.transpose(value)[:, 0:lanes]
    for copies in started:
        sent(copies)

    for slot in range(3):
        x_copy(gx.after(slot + 1), slot).wait_send()
    for step in range(1, 4):
        for low in range(2):
            y_copy(step, low).wait_send()
    for quarter in range(4):
        crossing(quarter).wait_send()


def main(order, points, targets, coeffs, block_inverse, collective_id):
    i16, bf16 = jnp.int16, jnp.bfloat16
    return pl.pallas_call(
        main_kernel,
        out_shape=jax.ShapeDtypeStruct((128, coeffs.shape[2]), F32),
        in_specs=[pl.BlockSpec(memory_space=pltpu.SMEM), VMEM, VMEM, VMEM, VMEM],
        out_specs=VMEM,
        scratch_shapes=[
            pltpu.VMEM((16, 16, 512), bf16),
            pltpu.VMEM((16, 8, 1024), F32),
            pltpu.VMEM((16, 16, 512), bf16),
            pltpu.VMEM((16, 512), bf16),
            pltpu.VMEM((2, 2, 4, 2, 2, 32, 1024), bf16),
            pltpu.VMEM((1024, 1152), bf16),
            pltpu.VMEM((8, 384), F32),
            pltpu.VMEM((2, 4, 256, 1152), bf16),
            pltpu.VMEM((4, 2, 4, 256, 128), F32),
            pltpu.VMEM((8, 256, 128), F32),
            pltpu.VMEM((4, 2064, 128), i16),
            pltpu.VMEM((4, 2064, 128), i16),
            pltpu.VMEM((3, 1040, 128), i16),
            pltpu.VMEM((3, 1040, 128), i16),
            pltpu.VMEM((3, 2, 528, 128), i16),
            pltpu.VMEM((3, 2, 528, 128), i16),
            pltpu.VMEM((4, 256, 128), F32),
            pltpu.VMEM((4, 256, 128), F32),
            pltpu.VMEM((3, 272, 128), i16),
            pltpu.VMEM((3, 272, 128), i16),
            pltpu.VMEM((3, 272, 128), i16),
            pltpu.VMEM((3, 272, 128), i16),
            pltpu.VMEM((512, 128), F32),
            pltpu.VMEM((7, 80, 128), i16),
            pltpu.VMEM((7, 80, 128), i16),
            pltpu.VMEM((16, 8, 1024), F32),
            pltpu.VMEM((16, 8, 1024), F32),
            pltpu.VMEM((16, 80, 128), i16),
            pltpu.VMEM((16, 80, 128), i16),
            pltpu.VMEM((16, 80, 128), i16),
            pltpu.VMEM((16, 80, 128), i16),
            pltpu.VMEM((16, 80, 128), i16),
            pltpu.VMEM((2, 64, 1024), F32),
            pltpu.VMEM((64, 1024), F32),
            pltpu.VMEM((1024, 1024), bf16),
            pltpu.VMEM((1024, 1024), bf16),
            pltpu.VMEM((128, 1024), F32),
            DMA((160,)), DMA((160,)), DMA((4,)),
        ],
        compiler_params=pltpu.CompilerParams(collective_id=collective_id, has_side_effects=True, vmem_limit_bytes=56 * 2**20),
    )(order, points, targets, coeffs, block_inverse)


def on_device(points, targets, coeffs, block_inverse, block_order):
    blocks_here, per_col, _ = points.shape
    classes = targets.shape[2]
    deltas = main(block_order, points, targets, coeffs, block_inverse, 0)
    deltas = deltas.reshape(2, per_col, classes)

    block = lax.axis_index("row") * blocks_here + lax.broadcasted_iota(jnp.int32, (blocks_here, 1, 1), 0)
    current = coeffs
    for step in range(2):
        current = jnp.where(block == block_order[step], current + deltas[step][None], current)
    return current


def solution(mesh):
    placed = (
        P("row", "col", None),
        P("row", "col", None),
        P("row", "col", None),
        P("row", "col", None),
        P(),
    )
    return jax.shard_map(
        on_device, mesh=mesh, in_specs=placed, out_specs=P("row", "col", None), check_vma=False
    )
```

```python
import functools

import jax
import jax.numpy as jnp
from jax import lax
from jax.experimental import pallas as pl
from jax.experimental.pallas import tpu as pltpu
from jax.sharding import PartitionSpec as P

MESH = pl.DeviceIdType.MESH
ANY = pl.BlockSpec(memory_space=pl.ANY)
VMEM = pl.BlockSpec(memory_space=pltpu.VMEM)
DMA = pltpu.SemaphoreType.DMA

ridge_weight = 1.0


def place():
    row, col = lax.axis_index("row"), lax.axis_index("col")
    return col // 8, row // 8, (col // 2) % 4, row % 8, col % 2


def device(x, y, z, core):
    return (x % 2) * 8 + z, (x // 2) * 8 + y * 2 + core


class Group:
    def __init__(self, kind):
        x_hi, x_lo, y, z, core = place()
        row, col = lax.axis_index("row"), lax.axis_index("col")
        x = x_hi * 2 + x_lo
        self.size, self.me, self.at = {
            "row": (16, row, lambda i: (i, col)),
            "col": (16, col, lambda i: (row, i)),
            "x": (4, x, lambda i: device(i, y, z, core)),
            "y": (4, y, lambda i: device(x, i, z, core)),
            "z": (8, z, lambda i: device(x, y, i, core)),
            "core": (2, core, lambda i: device(x, y, z, i)),
        }[kind]

    def after(self, step):
        return lax.rem(self.me + step, self.size)

    def before(self, step):
        return lax.rem(self.me + self.size - step, self.size)


def signal_all(groups):
    barrier = pltpu.get_barrier_semaphore()
    for group in groups:
        for step in range(1, group.size):
            pl.semaphore_signal(barrier, inc=1, device_id=group.at(group.after(step)), device_id_type=MESH)


def wait_all(groups):
    pl.semaphore_wait(pltpu.get_barrier_semaphore(), sum(group.size - 1 for group in groups))


def send_all(group, source, target, send_sem, recv_sem):
    copies = []
    for step in range(1, group.size):
        to = group.after(step)
        out = pltpu.make_async_remote_copy(
            src_ref=source(to), dst_ref=target(group.me, step), send_sem=send_sem(step), recv_sem=recv_sem(step),
            device_id=group.at(to), device_id_type=MESH)
        out.start()
        back = pltpu.make_async_remote_copy(
            src_ref=source(to), dst_ref=target(group.before(step), step), send_sem=send_sem(step),
            recv_sem=recv_sem(step), device_id=group.at(to), device_id_type=MESH)
        copies.append((out, back))
    return copies


def arrived(copies):
    for _, back in copies:
        back.wait_recv()


def sent(copies):
    for out, _ in copies:
        out.wait_send()


F32 = jnp.float32
NT = (((1,), (1,)), ((), ()))
NN = (((1,), (0,)), ((), ()))
LIMIT = 32000.0
DOTS = dict(preferred_element_type=jnp.float32)


def code(pieces, slot):
    top = None
    for piece in pieces:
        size = jnp.abs(piece())
        top = size if top is None else jnp.maximum(top, size)
    top = jnp.max(top, axis=0, keepdims=True)
    level = jnp.ceil(jnp.log2(jnp.maximum(top, 1e-30)) * 16.0)
    row = jnp.broadcast_to(level, (16, 128))
    factor = LIMIT * jnp.exp2(row[0:1] * (-1.0 / 16.0))
    at = 0
    for piece in pieces:
        value = jnp.round(piece() * factor)
        rows = value.shape[0]
        slot[at:at + rows, :] = value.astype(jnp.int32).astype(jnp.int16)
        at += rows
    slot[at:at + 16, :] = row.astype(jnp.int32).astype(jnp.int16)


def wide(value):
    return value.astype(jnp.int32).astype(jnp.float32)


def scale_of(slot, rows):
    return jnp.exp2(wide(slot[rows:rows + 16, :])[0:1] * (1.0 / 16.0)) * (1.0 / LIMIT)


def decode(slot, rows):
    return wide(slot[0:rows, :]) * scale_of(slot, rows)


def squares_of(rows):
    value = rows.astype(F32)
    return jnp.sum(value * value, axis=1, keepdims=True)


def halves(value):
    high = value.astype(jnp.bfloat16)
    return high, (value - high.astype(F32)).astype(jnp.bfloat16)


def turn(block):
    rows, lanes = block.shape
    if lanes < 128:
        block = jnp.concatenate([block, jnp.zeros((rows, 128 - lanes), block.dtype)], axis=1)
    return jnp.transpose(block)


def main_kernel(order, points_in, targets_in, coeffs_in, block_inverse_in, out_1, out_2, hit,
                points, targets, coeffs, block_inverse, offers, inverse, offers_in, chunk, full, weights, squares_row, tile, mine, apart, theirs, core_in, x_out, x_in, y_out, y_in, u, v,
                y_out_2, y_in_2, x_out_2, x_in_2, z_sum, z_out, z_in, inverse_in, inverse_all, wanted, wanted_in, res_all,
                delta_all, last_all, res, delta, near_high, near_low, linked, send_sems, recv_sems, own_sems, load_sems):
    x_hi, x_lo, y, z, core = place()
    x = x_hi * 2 + x_lo
    classes = coeffs.shape[2]
    blocks_here = points.shape[0]
    owner, local = [order[t] // blocks_here for t in range(2)], [order[t] % blocks_here for t in range(2)]
    kinds = {kind: Group(kind) for kind in ("row", "col", "x", "y", "z", "core")}
    gx, gy, gz, gc, gr = (kinds[k] for k in ("x", "y", "z", "core", "row"))
    signal_all([gr, kinds["col"], gx])
    loads = [
        pltpu.make_async_copy(source, target, load_sems.at[i]) for i, (source, target) in enumerate((
            (points_in, points), (coeffs_in, coeffs), (targets_in, targets), (block_inverse_in, block_inverse)))
    ]
    for load in loads:
        load.start()
    for t in range(2):
        for b in range(blocks_here):
            here = jnp.where(gr.me * blocks_here + b == order[t], 1.0, 0.0)
            hit[t * 8 + b:t * 8 + b + 1, :] = jnp.full((1, 128), here, F32)
    loads[0].wait()
    for block in range(2):
        for q in range(8):
            offers[block * 8 + q] = points[local[block], (q // 2) * 16:(q // 2) * 16 + 16, (q % 2) * 512:(q % 2) * 512 + 512]
    wait_all([gr, kinds["col"], gx])
    next_sem = [0]
    started = []

    def take(count):
        next_sem[0] += count
        return next_sem[0] - count

    def send(group, source, target):
        base = take(group.size - 1)
        copies = send_all(group, source, target, lambda s: send_sems.at[base + s - 1], lambda s: recv_sems.at[base + s - 1])
        started.append(copies)
        return copies

    own_offer = pltpu.make_async_copy(offers.at[gr.me], offers_in.at[gr.me], own_sems.at[0])
    own_offer.start()
    offered = send(gr, lambda i: offers.at[i], lambda i, s: offers_in.at[i])
    loads[1].wait()
    for a in range(3):
        span = slice(a * 128, a * 128 + 128)
        squares_row[:, span] = turn(jnp.broadcast_to(squares_of(points[2 * a:2 * a + 2].reshape(128, 1024)), (128, 128)))[0:8]
        for b in range(8):
            high, low = halves(turn(coeffs[2 * a:2 * a + 2, :, b * 128:min(b * 128 + 128, classes)].reshape(128, -1)))
            weights[b * 128:b * 128 + 128, a * 128:a * 128 + 128] = high
            weights[b * 128:b * 128 + 128, a * 128 + 384:a * 128 + 512] = low
            weights[b * 128:b * 128 + 128, a * 128 + 768:a * 128 + 896] = high
    loads[2].wait()
    for b in range(8):
        lanes = slice(b * 128, min(b * 128 + 128, classes))
        block = turn(jnp.concatenate([
            targets[local[t], :, lanes].astype(F32) - ridge_weight * coeffs[local[t], :, lanes] for t in range(2)
        ], axis=0))
        code([lambda: block[0:64]], wanted.at[2 * b])
        code([lambda: block[64:128]], wanted.at[2 * b + 1])
    loads[3].wait()
    for q in range(16):
        inverse[q] = block_inverse[local[q // 8], (q % 8) * 8:(q % 8) * 8 + 8, :]
    own_offer.wait()
    arrived(offered)
    my_owner = jnp.where(x_lo == 0, owner[0], owner[1])
    chunk[...] = offers_in[my_owner]

    def piece(i):
        quarter, lanes = i // 2, i % 2
        return full.at[x_lo, x_hi, y, core, quarter // 2, pl.ds(pl.multiple_of((quarter % 2) * 16, 16), 16),
                       pl.ds(pl.multiple_of(lanes * 512, 512), 512)]

    own_chunk = pltpu.make_async_copy(chunk, piece(z), own_sems.at[3])
    own_chunk.start()
    along_z = send(gz, lambda i: chunk, lambda i, s: piece(i))
    own_chunk.wait()
    arrived(along_z)
    x_first = send(gx, lambda i: full.at[x_lo, x_hi, y, core, 0], lambda i, s: full.at[i % 2, i // 2, y, core, 0])
    y_first = send(gy, lambda i: full.at[x_lo, x_hi, y, core, 1], lambda i, s: full.at[x_lo, x_hi, i, core, 1])
    arrived(x_first)
    y_last = send(gy, lambda i: full.at[:, :, y, core, 0], lambda i, s: full.at[:, :, i, core, 0])
    arrived(y_first)
    x_last = send(gx, lambda i: full.at[x_lo, x_hi, :, core, 1], lambda i, s: full.at[i % 2, i // 2, :, core, 1])
    own_inverse = pltpu.make_async_copy(inverse.at[gr.me], inverse_in.at[gr.me], own_sems.at[1])
    own_inverse.start()
    inverse_sent = send(gr, lambda i: inverse.at[i], lambda i, s: inverse_in.at[i])
    arrived(y_last)
    across_0 = send(gc, lambda i: full.at[:, :, :, core, 0], lambda i, s: full.at[:, :, :, i, 0])
    arrived(x_last)
    across_1 = send(gc, lambda i: full.at[:, :, :, core, 1], lambda i, s: full.at[:, :, :, i, 1])

    def near(for_core, i):
        rows = jnp.concatenate([
            full[block, i // 2, (i % 2) * 2 + t, for_core].reshape(64, 1024) for t in range(2) for block in range(2)
        ], axis=0)
        inner = lax.dot_general(rows, points[...].reshape(384, 1024), NT, **DOTS)
        distance = squares_of(rows) + squares_row[0:1, :] - 2.0 * inner
        high, low = halves(jnp.exp(-distance * (0.5 / 1024)))
        tile[for_core, i, :, 0:384] = high
        tile[for_core, i, :, 384:768] = high
        tile[for_core, i, :, 768:1152] = low

    def own_tile(i, carry):
        near(core, i)
        return carry

    def other_tile(i, carry):
        near(1 - core, i)
        return carry

    lax.fori_loop(0, 4, own_tile, 0)
    own_inverse.wait()
    arrived(inverse_sent)
    inverse_all[gr.me] = inverse_in[my_owner]
    inverse_spread = send(gr, lambda i: inverse_all.at[gr.me], lambda i, s: inverse_all.at[i])
    wanted_sent = send(gr, lambda i: wanted.at[i], lambda i, s: wanted_in.at[i])
    arrived(across_0)
    arrived(across_1)
    lax.fori_loop(0, 4, other_tile, 0)

    crossing_base = take(4)
    x_base, y_base = take(3), take(6)

    def crossing(quarter):
        return pltpu.make_async_remote_copy(
            src_ref=theirs.at[quarter], dst_ref=core_in.at[quarter], send_sem=send_sems.at[crossing_base + quarter],
            recv_sem=recv_sems.at[crossing_base + quarter], device_id=gc.at(gc.after(1)), device_id_type=MESH)

    def products(for_core, quarter):
        part = weights[quarter * 256:quarter * 256 + 256, :]
        return lax.dot_general(part, tile[for_core].reshape(1024, 1152), NT, **DOTS)

    def summed(quarter, to_hi, to_y):
        return lambda: mine[quarter, to_hi, to_y]

    def x_copy(to, slot):
        return pltpu.make_async_remote_copy(
            src_ref=x_out.at[slot], dst_ref=x_in.at[slot], send_sem=send_sems.at[x_base + slot],
            recv_sem=recv_sems.at[x_base + slot], device_id=gx.at(to), device_id_type=MESH)

    def y_copy(step, low):
        return pltpu.make_async_remote_copy(
            src_ref=y_out.at[step - 1, low], dst_ref=y_in.at[step - 1, low],
            send_sem=send_sems.at[y_base + 2 * (step - 1) + low], recv_sem=recv_sems.at[y_base + 2 * (step - 1) + low],
            device_id=gy.at(gy.after(step)), device_id_type=MESH)

    def leave_quarter(quarter):
        low, half = quarter // 2, quarter % 2
        crossing(quarter).wait_recv()
        factor = scale_of(core_in.at[quarter], 2048)
        for i in range(8):
            mine[quarter, i // 4, i % 4] += wide(core_in[quarter, i * 256:i * 256 + 256, :]) * factor
        if half == 0:
            for high in range(2):
                to = high * 2 + low

                @pl.when(to != x)
                def _(high=high, to=to):
                    slot = lax.rem(to + 3 - x, 4)
                    code([summed(quarter, high, t) for t in range(4)], x_out.at[slot])
                    x_copy(to, slot).start()
        else:
            for step in range(1, 4):
                code([summed(quarter, t, gy.after(step)) for t in range(2)], y_out.at[step - 1, low])
                y_copy(step, low).start()

    for quarter in range(4):
        result = products(1 - core, quarter)
        for i in range(8):
            apart[i] = result[:, i * 128:i * 128 + 128]
        code([lambda i=i: apart[i] for i in range(8)], theirs.at[quarter])
        crossing(quarter).start()
    for quarter in range(4):
        result = products(core, quarter)
        for i in range(8):
            mine[quarter, i // 4, i % 4] = result[:, i * 128:i * 128 + 128]
        leave_quarter(quarter)

    for slot in range(3):
        x_copy(gx.after(slot + 1), slot).wait_recv()
    for t in range(4):
        value = summed(2 * x_lo, x_hi, t)()
        for i in range(3):
            value += wide(x_in[i, t * 256:t * 256 + 256, :]) * scale_of(x_in.at[i], 1024)
        u[t] = value
    for step in range(1, 4):
        code([lambda: u[gy.after(step)]], y_out_2.at[step - 1])
    y_last = send(gy, lambda i: y_out_2.at[lax.rem(i + 3 - y, 4)], lambda i, s: y_in_2.at[s - 1])
    for step in range(1, 4):
        for low in range(2):
            y_copy(step, low).wait_recv()
    for t in range(4):
        value = summed(2 * (t % 2) + 1, t // 2, y)()
        for i in range(3):
            slot = y_in.at[i, t % 2]
            value += wide(y_in[i, t % 2, (t // 2) * 256:(t // 2) * 256 + 256, :]) * scale_of(slot, 512)
        v[t] = value
    for step in range(1, 4):
        code([lambda: v[gx.after(step)]], x_out_2.at[step - 1])
    x_last = send(gx, lambda i: x_out_2.at[lax.rem(i + 3 - x, 4)], lambda i, s: x_in_2.at[s - 1])
    arrived(y_last)
    value = u[y]
    for i in range(3):
        value += decode(y_in_2.at[i], 256)
    z_sum[0:256, :] = value
    arrived(x_last)
    value = v[x]
    for i in range(3):
        value += decode(x_in_2.at[i], 256)
    z_sum[256:512, :] = value

    def slab(i):
        return z_sum[pl.ds(pl.multiple_of(i * 64, 64), 64), :]

    for step in range(1, 8):
        code([lambda: slab(gz.after(step))], z_out.at[step - 1])
    to_z = send(gz, lambda i: z_out.at[lax.rem(i + 7 - z, 8)], lambda i, s: z_in.at[s - 1])
    first = full[0].reshape(1024, 1024)
    lengths = [
        jnp.transpose(jnp.broadcast_to(squares_of(full[0, t // 4, t % 4].reshape(128, 1024)), (128, 128)))[0:1, :]
        for t in range(8)
    ]
    lengths = jnp.concatenate(lengths, axis=1)
    for t in range(4):
        rows = full[1, t // 2, (t % 2) * 2:(t % 2) * 2 + 2].reshape(256, 1024)
        inner = lax.dot_general(rows, first, NT, **DOTS)
        high, low = halves(jnp.exp(-(squares_of(rows) + lengths - 2.0 * inner) * (0.5 / 1024)))
        near_high[t * 256:t * 256 + 256, :] = high
        near_low[t * 256:t * 256 + 256, :] = low

    left = lax.broadcasted_iota(jnp.int32, (64, 128), 1) < 64
    wanted_in[gr.me] = wanted[gr.me]
    arrived(wanted_sent)
    goal = jnp.where(left, decode(wanted_in[owner[0]], 64), decode(wanted_in[owner[1]], 64))
    arrived(to_z)
    value = slab(z)
    for i in range(7):
        value += decode(z_in.at[i], 64)
    residual = goal - value

    def spread(group, slots, value):
        code([lambda: value], slots.at[group.me])
        return send(group, lambda i: slots.at[group.me], lambda i, s: slots.at[i])

    def flip(value):
        return pltpu.roll(value, 64, 1)

    copies = spread(kinds["col"], res_all, residual)
    arrived(inverse_spread)
    rows_here = inverse_all[...].reshape(128, 1024)
    high, low = halves(rows_here)
    across = lax.dot_general(jnp.concatenate([high, low], axis=0), near_high[...], NN, **DOTS)
    linked[...] = across[0:128] + across[128:256] + lax.dot_general(high, near_low[...], NN, **DOTS)
    arrived(copies)
    for t in range(8):
        even, odd = decode(res_all.at[2 * t], 64), decode(res_all.at[2 * t + 1], 64)
        res[0, :, t * 128:t * 128 + 128] = jnp.where(left, even, flip(odd))
        res[1, :, t * 128:t * 128 + 128] = jnp.where(left, flip(even), odd)
    change_1 = lax.dot_general(res[0], rows_here, NT, precision=lax.Precision.HIGHEST, **DOTS)
    copies = spread(kinds["col"], delta_all, change_1)
    change_2 = lax.dot_general(res[1], rows_here, NT, precision=lax.Precision.HIGHEST, **DOTS)
    arrived(copies)
    for t in range(8):
        even, odd = decode(delta_all.at[2 * t], 64), decode(delta_all.at[2 * t + 1], 64)
        delta[:, t * 128:t * 128 + 128] = jnp.where(left, even, flip(odd))
    change_2 -= lax.dot_general(delta[...], linked[...], NT, precision=lax.Precision.HIGHEST, **DOTS)
    copies = spread(gr, last_all, jnp.where(left, change_1, change_2))
    arrived(copies)
    for t in range(8):
        value = jnp.concatenate([decode(last_all.at[2 * t], 64), decode(last_all.at[2 * t + 1], 64)], axis=0)
        lanes = min(128, classes - t * 128)
        value = jnp.transpose(value)
        out_1[:, t * 128:t * 128 + lanes] = value[0:64, 0:lanes]
        out_2[:, t * 128:t * 128 + lanes] = value[64:128, 0:lanes]
    for copies in started:
        sent(copies)

    for slot in range(3):
        x_copy(gx.after(slot + 1), slot).wait_send()
    for step in range(1, 4):
        for low in range(2):
            y_copy(step, low).wait_send()
    for quarter in range(4):
        crossing(quarter).wait_send()


def main(order, points, targets, coeffs, block_inverse, collective_id):
    i16, bf16 = jnp.int16, jnp.bfloat16
    return pl.pallas_call(
        main_kernel,
        out_shape=[jax.ShapeDtypeStruct((64, coeffs.shape[2]), F32)] * 2 + [jax.ShapeDtypeStruct((16, 128), F32)],
        in_specs=[pl.BlockSpec(memory_space=pltpu.SMEM), ANY, ANY, ANY, ANY],
        out_specs=[VMEM] * 3,
        scratch_shapes=[
            pltpu.VMEM(points.shape, bf16),
            pltpu.VMEM(targets.shape, bf16),
            pltpu.VMEM(coeffs.shape, F32),
            pltpu.VMEM(block_inverse.shape, F32),
            pltpu.VMEM((16, 16, 512), bf16),
            pltpu.VMEM((16, 8, 1024), F32),
            pltpu.VMEM((16, 16, 512), bf16),
            pltpu.VMEM((16, 512), bf16),
            pltpu.VMEM((2, 2, 4, 2, 2, 32, 1024), bf16),
            pltpu.VMEM((1024, 1152), bf16),
            pltpu.VMEM((8, 384), F32),
            pltpu.VMEM((2, 4, 256, 1152), bf16),
            pltpu.VMEM((4, 2, 4, 256, 128), F32),
            pltpu.VMEM((8, 256, 128), F32),
            pltpu.VMEM((4, 2064, 128), i16),
            pltpu.VMEM((4, 2064, 128), i16),
            pltpu.VMEM((3, 1040, 128), i16),
            pltpu.VMEM((3, 1040, 128), i16),
            pltpu.VMEM((3, 2, 528, 128), i16),
            pltpu.VMEM((3, 2, 528, 128), i16),
            pltpu.VMEM((4, 256, 128), F32),
            pltpu.VMEM((4, 256, 128), F32),
            pltpu.VMEM((3, 272, 128), i16),
            pltpu.VMEM((3, 272, 128), i16),
            pltpu.VMEM((3, 272, 128), i16),
            pltpu.VMEM((3, 272, 128), i16),
            pltpu.VMEM((512, 128), F32),
            pltpu.VMEM((7, 80, 128), i16),
            pltpu.VMEM((7, 80, 128), i16),
            pltpu.VMEM((16, 8, 1024), F32),
            pltpu.VMEM((16, 8, 1024), F32),
            pltpu.VMEM((16, 80, 128), i16),
            pltpu.VMEM((16, 80, 128), i16),
            pltpu.VMEM((16, 80, 128), i16),
            pltpu.VMEM((16, 80, 128), i16),
            pltpu.VMEM((16, 80, 128), i16),
            pltpu.VMEM((2, 64, 1024), F32),
            pltpu.VMEM((64, 1024), F32),
            pltpu.VMEM((1024, 1024), bf16),
            pltpu.VMEM((1024, 1024), bf16),
            pltpu.VMEM((128, 1024), F32),
            DMA((160,)), DMA((160,)), DMA((4,)), DMA((4,)),
        ],
        compiler_params=pltpu.CompilerParams(collective_id=collective_id, has_side_effects=True, vmem_limit_bytes=56 * 2**20),
    )(order, points, targets, coeffs, block_inverse)


def on_device(points, targets, coeffs, block_inverse, block_order):
    blocks_here = points.shape[0]
    change_1, change_2, hit = main(block_order, points, targets, coeffs, block_inverse, 0)
    hit = hit.reshape(2, 8, 128)[:, :blocks_here, 0:1, None] > 0
    return jnp.where(hit[0], coeffs + change_1[None], jnp.where(hit[1], coeffs + change_2[None], coeffs))


def solution(mesh):
    placed = (
        P("row", "col", None),
        P("row", "col", None),
        P("row", "col", None),
        P("row", "col", None),
        P(),
    )
    return jax.shard_map(
        on_device, mesh=mesh, in_specs=placed, out_specs=P("row", "col", None), check_vma=False
    )
```

```python
import functools

import jax
import jax.numpy as jnp
from jax import lax
from jax.experimental import pallas as pl
from jax.experimental.pallas import tpu as pltpu
from jax.sharding import PartitionSpec as P

MESH = pl.DeviceIdType.MESH
ANY = pl.BlockSpec(memory_space=pl.ANY)
VMEM = pl.BlockSpec(memory_space=pltpu.VMEM)
DMA = pltpu.SemaphoreType.DMA

ridge_weight = 1.0


def place():
    row, col = lax.axis_index("row"), lax.axis_index("col")
    return col // 8, row // 8, (col // 2) % 4, row % 8, col % 2


def device(x, y, z, core):
    return (x % 2) * 8 + z, (x // 2) * 8 + y * 2 + core


class Group:
    def __init__(self, kind):
        x_hi, x_lo, y, z, core = place()
        row, col = lax.axis_index("row"), lax.axis_index("col")
        x = x_hi * 2 + x_lo
        self.size, self.me, self.at = {
            "row": (16, row, lambda i: (i, col)),
            "col": (16, col, lambda i: (row, i)),
            "x": (4, x, lambda i: device(i, y, z, core)),
            "y": (4, y, lambda i: device(x, i, z, core)),
            "z": (8, z, lambda i: device(x, y, i, core)),
            "core": (2, core, lambda i: device(x, y, z, i)),
        }[kind]

    def after(self, step):
        return lax.rem(self.me + step, self.size)

    def before(self, step):
        return lax.rem(self.me + self.size - step, self.size)


def signal_all(groups):
    barrier = pltpu.get_barrier_semaphore()
    for group in groups:
        for step in range(1, group.size):
            pl.semaphore_signal(barrier, inc=1, device_id=group.at(group.after(step)), device_id_type=MESH)


def wait_all(groups):
    pl.semaphore_wait(pltpu.get_barrier_semaphore(), sum(group.size - 1 for group in groups))


def send_all(group, source, target, send_sem, recv_sem):
    copies = []
    turn_of = min(group.size, 8)
    far_first = sorted(range(1, group.size), key=lambda step: -min(step % turn_of, turn_of - step % turn_of))
    for step in far_first:
        to = group.after(step)
        out = pltpu.make_async_remote_copy(
            src_ref=source(to), dst_ref=target(group.me, step), send_sem=send_sem(step), recv_sem=recv_sem(step),
            device_id=group.at(to), device_id_type=MESH)
        out.start()
        back = pltpu.make_async_remote_copy(
            src_ref=source(to), dst_ref=target(group.before(step), step), send_sem=send_sem(step),
            recv_sem=recv_sem(step), device_id=group.at(to), device_id_type=MESH)
        copies.append((out, back))
    return copies


def arrived(copies):
    for _, back in copies:
        back.wait_recv()


def sent(copies):
    for out, _ in copies:
        out.wait_send()


F32 = jnp.float32
NT = (((1,), (1,)), ((), ()))
NN = (((1,), (0,)), ((), ()))
LIMIT = 32000.0
DOTS = dict(preferred_element_type=jnp.float32)


def code(pieces, slot):
    top = None
    for piece in pieces:
        size = jnp.abs(piece())
        top = size if top is None else jnp.maximum(top, size)
    top = jnp.max(top, axis=0, keepdims=True)
    level = jnp.ceil(jnp.log2(jnp.maximum(top, 1e-30)) * 16.0)
    row = jnp.broadcast_to(level, (16, 128))
    factor = LIMIT * jnp.exp2(row[0:1] * (-1.0 / 16.0))
    at = 0
    for piece in pieces:
        value = jnp.round(piece() * factor)
        rows = value.shape[0]
        slot[at:at + rows, :] = value.astype(jnp.int32).astype(jnp.int16)
        at += rows
    slot[at:at + 16, :] = row.astype(jnp.int32).astype(jnp.int16)


def wide(value):
    return value.astype(jnp.int32).astype(jnp.float32)


def scale_of(slot, rows):
    return jnp.exp2(wide(slot[rows:rows + 16, :])[0:1] * (1.0 / 16.0)) * (1.0 / LIMIT)


def decode(slot, rows):
    return wide(slot[0:rows, :]) * scale_of(slot, rows)


def squares_of(rows):
    value = rows.astype(F32)
    return jnp.sum(value * value, axis=1, keepdims=True)


def halves(value):
    high = value.astype(jnp.bfloat16)
    return high, (value - high.astype(F32)).astype(jnp.bfloat16)


def turn(block):
    rows, lanes = block.shape
    if lanes < 128:
        block = jnp.concatenate([block, jnp.zeros((rows, 128 - lanes), block.dtype)], axis=1)
    return jnp.transpose(block)


def main_kernel(order, points_in, targets_in, coeffs_in, block_inverse_in, out_1, out_2, hit,
                points, targets, coeffs, block_inverse, offers, inverse, offers_in, chunk, full, weights, squares_row, tile, mine, apart, theirs, core_in, x_out, x_in, y_out, y_in, u, v,
                y_out_2, y_in_2, x_out_2, x_in_2, z_sum, z_out, z_in, inverse_in, inverse_all, wanted, wanted_in, res_all,
                delta_all, last_all, res, delta, near_high, near_low, linked, send_sems, recv_sems, own_sems, load_sems):
    x_hi, x_lo, y, z, core = place()
    x = x_hi * 2 + x_lo
    classes = coeffs.shape[2]
    blocks_here = points.shape[0]
    owner, local = [order[t] // blocks_here for t in range(2)], [order[t] % blocks_here for t in range(2)]
    kinds = {kind: Group(kind) for kind in ("row", "col", "x", "y", "z", "core")}
    gx, gy, gz, gc, gr = (kinds[k] for k in ("x", "y", "z", "core", "row"))
    signal_all([gr, kinds["col"], gx])
    loads = [
        pltpu.make_async_copy(source, target, load_sems.at[i]) for i, (source, target) in enumerate((
            (points_in, points), (coeffs_in, coeffs), (targets_in, targets), (block_inverse_in, block_inverse)))
    ]
    for load in loads:
        load.start()
    for t in range(2):
        for b in range(blocks_here):
            here = jnp.where(gr.me * blocks_here + b == order[t], 1.0, 0.0)
            hit[t * 8 + b:t * 8 + b + 1, :] = jnp.full((1, 128), here, F32)
    loads[0].wait()
    for block in range(2):
        for q in range(8):
            offers[block * 8 + q] = points[local[block], (q // 2) * 16:(q // 2) * 16 + 16, (q % 2) * 512:(q % 2) * 512 + 512]
    wait_all([gr, kinds["col"], gx])
    next_sem = [0]
    started = []

    def take(count):
        next_sem[0] += count
        return next_sem[0] - count

    def send(group, source, target):
        base = take(group.size - 1)
        copies = send_all(group, source, target, lambda s: send_sems.at[base + s - 1], lambda s: recv_sems.at[base + s - 1])
        started.append(copies)
        return copies

    own_offer = pltpu.make_async_copy(offers.at[gr.me], offers_in.at[gr.me], own_sems.at[0])
    own_offer.start()
    offered = send(gr, lambda i: offers.at[i], lambda i, s: offers_in.at[i])
    loads[1].wait()
    for a in range(3):
        span = slice(a * 128, a * 128 + 128)
        squares_row[:, span] = turn(jnp.broadcast_to(squares_of(points[2 * a:2 * a + 2].reshape(128, 1024)), (128, 128)))[0:8]
        for b in range(8):
            high, low = halves(turn(coeffs[2 * a:2 * a + 2, :, b * 128:min(b * 128 + 128, classes)].reshape(128, -1)))
            weights[b * 128:b * 128 + 128, a * 128:a * 128 + 128] = high
            weights[b * 128:b * 128 + 128, a * 128 + 384:a * 128 + 512] = low
            weights[b * 128:b * 128 + 128, a * 128 + 768:a * 128 + 896] = high
    loads[2].wait()
    for b in range(8):
        lanes = slice(b * 128, min(b * 128 + 128, classes))
        block = turn(jnp.concatenate([
            targets[local[t], :, lanes].astype(F32) - ridge_weight * coeffs[local[t], :, lanes] for t in range(2)
        ], axis=0))
        code([lambda: block[0:64]], wanted.at[2 * b])
        code([lambda: block[64:128]], wanted.at[2 * b + 1])
    loads[3].wait()
    for q in range(16):
        inverse[q] = block_inverse[local[q // 8], (q % 8) * 8:(q % 8) * 8 + 8, :]
    own_offer.wait()
    arrived(offered)
    my_owner = jnp.where(x_lo == 0, owner[0], owner[1])
    chunk[...] = offers_in[my_owner]

    def piece(i):
        quarter, lanes = i // 2, i % 2
        return full.at[x_lo, x_hi, y, core, quarter // 2, pl.ds(pl.multiple_of((quarter % 2) * 16, 16), 16),
                       pl.ds(pl.multiple_of(lanes * 512, 512), 512)]

    own_chunk = pltpu.make_async_copy(chunk, piece(z), own_sems.at[3])
    own_chunk.start()
    along_z = send(gz, lambda i: chunk, lambda i, s: piece(i))
    own_chunk.wait()
    arrived(along_z)
    x_first = send(gx, lambda i: full.at[x_lo, x_hi, y, core, 0], lambda i, s: full.at[i % 2, i // 2, y, core, 0])
    y_first = send(gy, lambda i: full.at[x_lo, x_hi, y, core, 1], lambda i, s: full.at[x_lo, x_hi, i, core, 1])
    arrived(x_first)
    y_last = send(gy, lambda i: full.at[:, :, y, core, 0], lambda i, s: full.at[:, :, i, core, 0])
    arrived(y_first)
    x_last = send(gx, lambda i: full.at[x_lo, x_hi, :, core, 1], lambda i, s: full.at[i % 2, i // 2, :, core, 1])
    own_inverse = pltpu.make_async_copy(inverse.at[gr.me], inverse_in.at[gr.me], own_sems.at[1])
    own_inverse.start()
    inverse_sent = send(gr, lambda i: inverse.at[i], lambda i, s: inverse_in.at[i])
    arrived(y_last)
    across_0 = send(gc, lambda i: full.at[:, :, :, core, 0], lambda i, s: full.at[:, :, :, i, 0])
    arrived(x_last)
    across_1 = send(gc, lambda i: full.at[:, :, :, core, 1], lambda i, s: full.at[:, :, :, i, 1])

    def near(for_core, i):
        rows = jnp.concatenate([
            full[block, i // 2, (i % 2) * 2 + t, for_core].reshape(64, 1024) for t in range(2) for block in range(2)
        ], axis=0)
        inner = lax.dot_general(rows, points[...].reshape(384, 1024), NT, **DOTS)
        distance = squares_of(rows) + squares_row[0:1, :] - 2.0 * inner
        high, low = halves(jnp.exp(-distance * (0.5 / 1024)))
        tile[for_core, i, :, 0:384] = high
        tile[for_core, i, :, 384:768] = high
        tile[for_core, i, :, 768:1152] = low

    def own_tile(i, carry):
        near(core, i)
        return carry

    def other_tile(i, carry):
        near(1 - core, i)
        return carry

    lax.fori_loop(0, 4, own_tile, 0)
    own_inverse.wait()
    arrived(inverse_sent)
    inverse_all[gr.me] = inverse_in[my_owner]
    inverse_spread = send(gr, lambda i: inverse_all.at[gr.me], lambda i, s: inverse_all.at[i])
    wanted_sent = send(gr, lambda i: wanted.at[i], lambda i, s: wanted_in.at[i])
    arrived(across_0)
    arrived(across_1)
    lax.fori_loop(0, 4, other_tile, 0)

    crossing_base = take(4)
    x_base, y_base = take(3), take(6)

    def crossing(quarter):
        return pltpu.make_async_remote_copy(
            src_ref=theirs.at[quarter], dst_ref=core_in.at[quarter], send_sem=send_sems.at[crossing_base + quarter],
            recv_sem=recv_sems.at[crossing_base + quarter], device_id=gc.at(gc.after(1)), device_id_type=MESH)

    def products(for_core, quarter):
        part = weights[quarter * 256:quarter * 256 + 256, :]
        return lax.dot_general(part, tile[for_core].reshape(1024, 1152), NT, **DOTS)

    def summed(quarter, to_hi, to_y):
        return lambda: mine[quarter, to_hi, to_y]

    def x_copy(to, slot):
        return pltpu.make_async_remote_copy(
            src_ref=x_out.at[slot], dst_ref=x_in.at[slot], send_sem=send_sems.at[x_base + slot],
            recv_sem=recv_sems.at[x_base + slot], device_id=gx.at(to), device_id_type=MESH)

    def y_copy(step, low):
        return pltpu.make_async_remote_copy(
            src_ref=y_out.at[step - 1, low], dst_ref=y_in.at[step - 1, low],
            send_sem=send_sems.at[y_base + 2 * (step - 1) + low], recv_sem=recv_sems.at[y_base + 2 * (step - 1) + low],
            device_id=gy.at(gy.after(step)), device_id_type=MESH)

    def leave_quarter(quarter):
        low, half = quarter // 2, quarter % 2
        crossing(quarter).wait_recv()
        factor = scale_of(core_in.at[quarter], 2048)
        for i in range(8):
            mine[quarter, i // 4, i % 4] += wide(core_in[quarter, i * 256:i * 256 + 256, :]) * factor
        if half == 0:
            for high in range(2):
                to = high * 2 + low

                @pl.when(to != x)
                def _(high=high, to=to):
                    slot = lax.rem(to + 3 - x, 4)
                    code([summed(quarter, high, t) for t in range(4)], x_out.at[slot])
                    x_copy(to, slot).start()
        else:
            for step in range(1, 4):
                code([summed(quarter, t, gy.after(step)) for t in range(2)], y_out.at[step - 1, low])
                y_copy(step, low).start()

    def cross_quarter(quarter):
        result = products(1 - core, quarter)
        for i in range(8):
            apart[i] = result[:, i * 128:i * 128 + 128]
        code([lambda i=i: apart[i] for i in range(8)], theirs.at[quarter])
        crossing(quarter).start()

    def own_quarter(quarter):
        result = products(core, quarter)
        for i in range(8):
            mine[quarter, i // 4, i % 4] = result[:, i * 128:i * 128 + 128]

    cross_quarter(0)
    own_quarter(0)
    for quarter in range(1, 4):
        cross_quarter(quarter)
        leave_quarter(quarter - 1)
        own_quarter(quarter)
    leave_quarter(3)

    for slot in range(3):
        x_copy(gx.after(slot + 1), slot).wait_recv()
    for t in range(4):
        value = summed(2 * x_lo, x_hi, t)()
        for i in range(3):
            value += wide(x_in[i, t * 256:t * 256 + 256, :]) * scale_of(x_in.at[i], 1024)
        u[t] = value
    for step in range(1, 4):
        code([lambda: u[gy.after(step)]], y_out_2.at[step - 1])
    y_last = send(gy, lambda i: y_out_2.at[lax.rem(i + 3 - y, 4)], lambda i, s: y_in_2.at[s - 1])
    for step in range(1, 4):
        for low in range(2):
            y_copy(step, low).wait_recv()
    for t in range(4):
        value = summed(2 * (t % 2) + 1, t // 2, y)()
        for i in range(3):
            slot = y_in.at[i, t % 2]
            value += wide(y_in[i, t % 2, (t // 2) * 256:(t // 2) * 256 + 256, :]) * scale_of(slot, 512)
        v[t] = value
    for step in range(1, 4):
        code([lambda: v[gx.after(step)]], x_out_2.at[step - 1])
    x_last = send(gx, lambda i: x_out_2.at[lax.rem(i + 3 - x, 4)], lambda i, s: x_in_2.at[s - 1])
    arrived(y_last)
    value = u[y]
    for i in range(3):
        value += decode(y_in_2.at[i], 256)
    z_sum[0:256, :] = value
    arrived(x_last)
    value = v[x]
    for i in range(3):
        value += decode(x_in_2.at[i], 256)
    z_sum[256:512, :] = value

    def slab(i):
        return z_sum[pl.ds(pl.multiple_of(i * 64, 64), 64), :]

    for step in range(1, 8):
        code([lambda: slab(gz.after(step))], z_out.at[step - 1])
    to_z = send(gz, lambda i: z_out.at[lax.rem(i + 7 - z, 8)], lambda i, s: z_in.at[s - 1])
    first = full[0].reshape(1024, 1024)
    lengths = [
        jnp.transpose(jnp.broadcast_to(squares_of(full[0, t // 4, t % 4].reshape(128, 1024)), (128, 128)))[0:1, :]
        for t in range(8)
    ]
    lengths = jnp.concatenate(lengths, axis=1)
    for t in range(4):
        rows = full[1, t // 2, (t % 2) * 2:(t % 2) * 2 + 2].reshape(256, 1024)
        inner = lax.dot_general(rows, first, NT, **DOTS)
        high, low = halves(jnp.exp(-(squares_of(rows) + lengths - 2.0 * inner) * (0.5 / 1024)))
        near_high[t * 256:t * 256 + 256, :] = high
        near_low[t * 256:t * 256 + 256, :] = low

    left = lax.broadcasted_iota(jnp.int32, (64, 128), 1) < 64
    wanted_in[gr.me] = wanted[gr.me]
    arrived(wanted_sent)
    goal = jnp.where(left, decode(wanted_in[owner[0]], 64), decode(wanted_in[owner[1]], 64))
    arrived(to_z)
    value = slab(z)
    for i in range(7):
        value += decode(z_in.at[i], 64)
    residual = goal - value

    def spread(group, slots, value):
        code([lambda: value], slots.at[group.me])
        return send(group, lambda i: slots.at[group.me], lambda i, s: slots.at[i])

    def flip(value):
        return pltpu.roll(value, 64, 1)

    copies = spread(kinds["col"], res_all, residual)
    arrived(inverse_spread)
    rows_here = inverse_all[...].reshape(128, 1024)
    high, low = halves(rows_here)
    across = lax.dot_general(jnp.concatenate([high, low], axis=0), near_high[...], NN, **DOTS)
    linked[...] = across[0:128] + across[128:256] + lax.dot_general(high, near_low[...], NN, **DOTS)
    arrived(copies)
    for t in range(8):
        even, odd = decode(res_all.at[2 * t], 64), decode(res_all.at[2 * t + 1], 64)
        res[0, :, t * 128:t * 128 + 128] = jnp.where(left, even, flip(odd))
        res[1, :, t * 128:t * 128 + 128] = jnp.where(left, flip(even), odd)
    change_1 = lax.dot_general(res[0], rows_here, NT, precision=lax.Precision.HIGHEST, **DOTS)
    copies = spread(kinds["col"], delta_all, change_1)
    change_2 = lax.dot_general(res[1], rows_here, NT, precision=lax.Precision.HIGHEST, **DOTS)
    arrived(copies)
    for t in range(8):
        even, odd = decode(delta_all.at[2 * t], 64), decode(delta_all.at[2 * t + 1], 64)
        delta[:, t * 128:t * 128 + 128] = jnp.where(left, even, flip(odd))
    change_2 -= lax.dot_general(delta[...], linked[...], NT, precision=lax.Precision.HIGHEST, **DOTS)
    copies = spread(gr, last_all, jnp.where(left, change_1, change_2))
    arrived(copies)
    for t in range(8):
        value = jnp.concatenate([decode(last_all.at[2 * t], 64), decode(last_all.at[2 * t + 1], 64)], axis=0)
        lanes = min(128, classes - t * 128)
        value = jnp.transpose(value)
        out_1[:, t * 128:t * 128 + lanes] = value[0:64, 0:lanes]
        out_2[:, t * 128:t * 128 + lanes] = value[64:128, 0:lanes]
    for copies in started:
        sent(copies)

    for slot in range(3):
        x_copy(gx.after(slot + 1), slot).wait_send()
    for step in range(1, 4):
        for low in range(2):
            y_copy(step, low).wait_send()
    for quarter in range(4):
        crossing(quarter).wait_send()


def main(order, points, targets, coeffs, block_inverse, collective_id):
    i16, bf16 = jnp.int16, jnp.bfloat16
    return pl.pallas_call(
        main_kernel,
        out_shape=[jax.ShapeDtypeStruct((64, coeffs.shape[2]), F32)] * 2 + [jax.ShapeDtypeStruct((16, 128), F32)],
        in_specs=[pl.BlockSpec(memory_space=pltpu.SMEM), ANY, ANY, ANY, ANY],
        out_specs=[VMEM] * 3,
        scratch_shapes=[
            pltpu.VMEM(points.shape, bf16),
            pltpu.VMEM(targets.shape, bf16),
            pltpu.VMEM(coeffs.shape, F32),
            pltpu.VMEM(block_inverse.shape, F32),
            pltpu.VMEM((16, 16, 512), bf16),
            pltpu.VMEM((16, 8, 1024), F32),
            pltpu.VMEM((16, 16, 512), bf16),
            pltpu.VMEM((16, 512), bf16),
            pltpu.VMEM((2, 2, 4, 2, 2, 32, 1024), bf16),
            pltpu.VMEM((1024, 1152), bf16),
            pltpu.VMEM((8, 384), F32),
            pltpu.VMEM((2, 4, 256, 1152), bf16),
            pltpu.VMEM((4, 2, 4, 256, 128), F32),
            pltpu.VMEM((8, 256, 128), F32),
            pltpu.VMEM((4, 2064, 128), i16),
            pltpu.VMEM((4, 2064, 128), i16),
            pltpu.VMEM((3, 1040, 128), i16),
            pltpu.VMEM((3, 1040, 128), i16),
            pltpu.VMEM((3, 2, 528, 128), i16),
            pltpu.VMEM((3, 2, 528, 128), i16),
            pltpu.VMEM((4, 256, 128), F32),
            pltpu.VMEM((4, 256, 128), F32),
            pltpu.VMEM((3, 272, 128), i16),
            pltpu.VMEM((3, 272, 128), i16),
            pltpu.VMEM((3, 272, 128), i16),
            pltpu.VMEM((3, 272, 128), i16),
            pltpu.VMEM((512, 128), F32),
            pltpu.VMEM((7, 80, 128), i16),
            pltpu.VMEM((7, 80, 128), i16),
            pltpu.VMEM((16, 8, 1024), F32),
            pltpu.VMEM((16, 8, 1024), F32),
            pltpu.VMEM((16, 80, 128), i16),
            pltpu.VMEM((16, 80, 128), i16),
            pltpu.VMEM((16, 80, 128), i16),
            pltpu.VMEM((16, 80, 128), i16),
            pltpu.VMEM((16, 80, 128), i16),
            pltpu.VMEM((2, 64, 1024), F32),
            pltpu.VMEM((64, 1024), F32),
            pltpu.VMEM((1024, 1024), bf16),
            pltpu.VMEM((1024, 1024), bf16),
            pltpu.VMEM((128, 1024), F32),
            DMA((160,)), DMA((160,)), DMA((4,)), DMA((4,)),
        ],
        compiler_params=pltpu.CompilerParams(collective_id=collective_id, has_side_effects=True, vmem_limit_bytes=56 * 2**20),
    )(order, points, targets, coeffs, block_inverse)


def on_device(points, targets, coeffs, block_inverse, block_order):
    blocks_here = points.shape[0]
    change_1, change_2, hit = main(block_order, points, targets, coeffs, block_inverse, 0)
    hit = hit.reshape(2, 8, 128)[:, :blocks_here, 0:1, None] > 0
    return jnp.where(hit[0], coeffs + change_1[None], jnp.where(hit[1], coeffs + change_2[None], coeffs))


def solution(mesh):
    placed = (
        P("row", "col", None),
        P("row", "col", None),
        P("row", "col", None),
        P("row", "col", None),
        P(),
    )
    return jax.shard_map(
        on_device, mesh=mesh, in_specs=placed, out_specs=P("row", "col", None), check_vma=False
    )
```

```python
import functools

import jax
import jax.numpy as jnp
from jax import lax
from jax.experimental import pallas as pl
from jax.experimental.pallas import tpu as pltpu
from jax.sharding import PartitionSpec as P

MESH = pl.DeviceIdType.MESH
ANY = pl.BlockSpec(memory_space=pl.ANY)
VMEM = pl.BlockSpec(memory_space=pltpu.VMEM)
DMA = pltpu.SemaphoreType.DMA

ridge_weight = 1.0


def place():
    row, col = lax.axis_index("row"), lax.axis_index("col")
    return col // 8, row // 8, (col // 2) % 4, row % 8, col % 2


def device(x, y, z, core):
    return (x % 2) * 8 + z, (x // 2) * 8 + y * 2 + core


class Group:
    def __init__(self, kind):
        x_hi, x_lo, y, z, core = place()
        row, col = lax.axis_index("row"), lax.axis_index("col")
        x = x_hi * 2 + x_lo
        self.size, self.me, self.at = {
            "row": (16, row, lambda i: (i, col)),
            "col": (16, col, lambda i: (row, i)),
            "x": (4, x, lambda i: device(i, y, z, core)),
            "y": (4, y, lambda i: device(x, i, z, core)),
            "z": (8, z, lambda i: device(x, y, i, core)),
            "core": (2, core, lambda i: device(x, y, z, i)),
        }[kind]

    def after(self, step):
        return lax.rem(self.me + step, self.size)

    def before(self, step):
        return lax.rem(self.me + self.size - step, self.size)


def far_first(size):
    turn_of = min(size, 8)
    return sorted(range(1, size), key=lambda step: -min(step % turn_of, turn_of - step % turn_of))


def signal_all(groups):
    barrier = pltpu.get_barrier_semaphore()
    for group in groups:
        for step in far_first(group.size):
            pl.semaphore_signal(barrier, inc=1, device_id=group.at(group.after(step)), device_id_type=MESH)


def wait_all(groups):
    pl.semaphore_wait(pltpu.get_barrier_semaphore(), sum(group.size - 1 for group in groups))


def send_all(group, source, target, send_sem, recv_sem):
    copies = []
    for step in far_first(group.size):
        to = group.after(step)
        out = pltpu.make_async_remote_copy(
            src_ref=source(to), dst_ref=target(group.me, step), send_sem=send_sem(step), recv_sem=recv_sem(step),
            device_id=group.at(to), device_id_type=MESH)
        out.start()
        back = pltpu.make_async_remote_copy(
            src_ref=source(to), dst_ref=target(group.before(step), step), send_sem=send_sem(step),
            recv_sem=recv_sem(step), device_id=group.at(to), device_id_type=MESH)
        copies.append((out, back))
    return copies


def arrived(copies):
    for _, back in copies:
        back.wait_recv()


def sent(copies):
    for out, _ in copies:
        out.wait_send()


F32 = jnp.float32
NT = (((1,), (1,)), ((), ()))
NN = (((1,), (0,)), ((), ()))
LIMIT = 32000.0
DOTS = dict(preferred_element_type=jnp.float32)


def code(pieces, slot):
    top = None
    for piece in pieces:
        size = jnp.abs(piece())
        top = size if top is None else jnp.maximum(top, size)
    top = jnp.max(top, axis=0, keepdims=True)
    level = jnp.ceil(jnp.log2(jnp.maximum(top, 1e-30)) * 16.0)
    row = jnp.broadcast_to(level, (16, 128))
    factor = LIMIT * jnp.exp2(row[0:1] * (-1.0 / 16.0))
    at = 0
    for piece in pieces:
        value = jnp.round(piece() * factor)
        rows = value.shape[0]
        slot[at:at + rows, :] = value.astype(jnp.int32).astype(jnp.int16)
        at += rows
    slot[at:at + 16, :] = row.astype(jnp.int32).astype(jnp.int16)


def wide(value):
    return value.astype(jnp.int32).astype(jnp.float32)


def scale_of(slot, rows):
    return jnp.exp2(wide(slot[rows:rows + 16, :])[0:1] * (1.0 / 16.0)) * (1.0 / LIMIT)


def decode(slot, rows):
    return wide(slot[0:rows, :]) * scale_of(slot, rows)


def squares_of(rows):
    value = rows.astype(F32)
    return jnp.sum(value * value, axis=1, keepdims=True)


def halves(value):
    high = value.astype(jnp.bfloat16)
    return high, (value - high.astype(F32)).astype(jnp.bfloat16)


def turn(block):
    rows, lanes = block.shape
    if lanes < 128:
        block = jnp.concatenate([block, jnp.zeros((rows, 128 - lanes), block.dtype)], axis=1)
    return jnp.transpose(block)


def main_kernel(order, points_in, targets_in, coeffs_in, block_inverse_in, out_1, out_2, hit,
                points, targets, coeffs, block_inverse, offers, inverse, offers_in, chunk, full, weights, squares_row, tile, mine, apart, theirs, core_in, x_out, x_in, y_out, y_in, u, v,
                y_out_2, y_in_2, x_out_2, x_in_2, z_sum, z_out, z_in, inverse_in, inverse_all, wanted, wanted_in, res_all,
                delta_all, last_all, res, delta, near_high, near_low, linked, send_sems, recv_sems, own_sems, load_sems):
    x_hi, x_lo, y, z, core = place()
    x = x_hi * 2 + x_lo
    classes = coeffs.shape[2]
    blocks_here = points.shape[0]
    owner, local = [order[t] // blocks_here for t in range(2)], [order[t] % blocks_here for t in range(2)]
    kinds = {kind: Group(kind) for kind in ("row", "col", "x", "y", "z", "core")}
    gx, gy, gz, gc, gr = (kinds[k] for k in ("x", "y", "z", "core", "row"))
    signal_all([gr, kinds["col"], gx])
    loads = [
        pltpu.make_async_copy(source, target, load_sems.at[i]) for i, (source, target) in enumerate((
            (points_in, points), (coeffs_in, coeffs), (targets_in, targets), (block_inverse_in, block_inverse)))
    ]
    for load in loads:
        load.start()
    for t in range(2):
        for b in range(blocks_here):
            here = jnp.where(gr.me * blocks_here + b == order[t], 1.0, 0.0)
            hit[t * 8 + b:t * 8 + b + 1, :] = jnp.full((1, 128), here, F32)
    loads[0].wait()
    for block in range(2):
        for q in range(8):
            offers[block * 8 + q] = points[local[block], (q // 2) * 16:(q // 2) * 16 + 16, (q % 2) * 512:(q % 2) * 512 + 512]
    wait_all([gr, kinds["col"], gx])
    next_sem = [0]
    started = []

    def take(count):
        next_sem[0] += count
        return next_sem[0] - count

    def send(group, source, target):
        base = take(group.size - 1)
        copies = send_all(group, source, target, lambda s: send_sems.at[base + s - 1], lambda s: recv_sems.at[base + s - 1])
        started.append(copies)
        return copies

    own_offer = pltpu.make_async_copy(offers.at[gr.me], offers_in.at[gr.me], own_sems.at[0])
    own_offer.start()
    offered = send(gr, lambda i: offers.at[i], lambda i, s: offers_in.at[i])
    loads[1].wait()
    for a in range(3):
        span = slice(a * 128, a * 128 + 128)
        squares_row[:, span] = turn(jnp.broadcast_to(squares_of(points[2 * a:2 * a + 2].reshape(128, 1024)), (128, 128)))[0:8]
        for b in range(8):
            high, low = halves(turn(coeffs[2 * a:2 * a + 2, :, b * 128:min(b * 128 + 128, classes)].reshape(128, -1)))
            weights[b * 128:b * 128 + 128, a * 128:a * 128 + 128] = high
            weights[b * 128:b * 128 + 128, a * 128 + 384:a * 128 + 512] = low
            weights[b * 128:b * 128 + 128, a * 128 + 768:a * 128 + 896] = high
    loads[2].wait()
    for b in range(8):
        lanes = slice(b * 128, min(b * 128 + 128, classes))
        block = turn(jnp.concatenate([
            targets[local[t], :, lanes].astype(F32) - ridge_weight * coeffs[local[t], :, lanes] for t in range(2)
        ], axis=0))
        code([lambda: block[0:64]], wanted.at[2 * b])
        code([lambda: block[64:128]], wanted.at[2 * b + 1])
    loads[3].wait()
    for q in range(16):
        inverse[q] = block_inverse[local[q // 8], (q % 8) * 8:(q % 8) * 8 + 8, :]
    own_offer.wait()
    arrived(offered)
    my_owner = jnp.where(x_lo == 0, owner[0], owner[1])
    chunk[...] = offers_in[my_owner]

    def piece(i):
        quarter, lanes = i // 2, i % 2
        return full.at[x_lo, x_hi, y, core, quarter // 2, pl.ds(pl.multiple_of((quarter % 2) * 16, 16), 16),
                       pl.ds(pl.multiple_of(lanes * 512, 512), 512)]

    own_chunk = pltpu.make_async_copy(chunk, piece(z), own_sems.at[3])
    own_chunk.start()
    along_z = send(gz, lambda i: chunk, lambda i, s: piece(i))
    own_chunk.wait()
    arrived(along_z)
    x_first = send(gx, lambda i: full.at[x_lo, x_hi, y, core, 0], lambda i, s: full.at[i % 2, i // 2, y, core, 0])
    y_first = send(gy, lambda i: full.at[x_lo, x_hi, y, core, 1], lambda i, s: full.at[x_lo, x_hi, i, core, 1])
    arrived(x_first)
    y_last = send(gy, lambda i: full.at[:, :, y, core, 0], lambda i, s: full.at[:, :, i, core, 0])
    arrived(y_first)
    x_last = send(gx, lambda i: full.at[x_lo, x_hi, :, core, 1], lambda i, s: full.at[i % 2, i // 2, :, core, 1])
    own_inverse = pltpu.make_async_copy(inverse.at[gr.me], inverse_in.at[gr.me], own_sems.at[1])
    own_inverse.start()
    inverse_sent = send(gr, lambda i: inverse.at[i], lambda i, s: inverse_in.at[i])
    arrived(y_last)
    across_0 = send(gc, lambda i: full.at[:, :, :, core, 0], lambda i, s: full.at[:, :, :, i, 0])
    arrived(x_last)
    across_1 = send(gc, lambda i: full.at[:, :, :, core, 1], lambda i, s: full.at[:, :, :, i, 1])

    def near(for_core, i):
        rows = jnp.concatenate([
            full[block, i // 2, (i % 2) * 2 + t, for_core].reshape(64, 1024) for t in range(2) for block in range(2)
        ], axis=0)
        inner = lax.dot_general(rows, points[...].reshape(384, 1024), NT, **DOTS)
        distance = squares_of(rows) + squares_row[0:1, :] - 2.0 * inner
        high, low = halves(jnp.exp(-distance * (0.5 / 1024)))
        tile[for_core, i, :, 0:384] = high
        tile[for_core, i, :, 384:768] = high
        tile[for_core, i, :, 768:1152] = low

    def own_tile(i, carry):
        near(core, i)
        return carry

    def other_tile(i, carry):
        near(1 - core, i)
        return carry

    lax.fori_loop(0, 4, own_tile, 0)
    own_inverse.wait()
    arrived(inverse_sent)
    inverse_all[gr.me] = inverse_in[my_owner]
    inverse_spread = send(gr, lambda i: inverse_all.at[gr.me], lambda i, s: inverse_all.at[i])
    wanted_sent = send(gr, lambda i: wanted.at[i], lambda i, s: wanted_in.at[i])
    arrived(across_0)
    arrived(across_1)
    lax.fori_loop(0, 4, other_tile, 0)

    crossing_base = take(4)
    x_base, y_base = take(3), take(6)

    def crossing(quarter):
        return pltpu.make_async_remote_copy(
            src_ref=theirs.at[quarter], dst_ref=core_in.at[quarter], send_sem=send_sems.at[crossing_base + quarter],
            recv_sem=recv_sems.at[crossing_base + quarter], device_id=gc.at(gc.after(1)), device_id_type=MESH)

    def products(for_core, quarter):
        part = weights[quarter * 256:quarter * 256 + 256, :]
        return lax.dot_general(part, tile[for_core].reshape(1024, 1152), NT, **DOTS)

    def summed(quarter, to_hi, to_y):
        return lambda: mine[quarter, to_hi, to_y]

    def x_copy(to, slot):
        return pltpu.make_async_remote_copy(
            src_ref=x_out.at[slot], dst_ref=x_in.at[slot], send_sem=send_sems.at[x_base + slot],
            recv_sem=recv_sems.at[x_base + slot], device_id=gx.at(to), device_id_type=MESH)

    def y_copy(step, low):
        return pltpu.make_async_remote_copy(
            src_ref=y_out.at[step - 1, low], dst_ref=y_in.at[step - 1, low],
            send_sem=send_sems.at[y_base + 2 * (step - 1) + low], recv_sem=recv_sems.at[y_base + 2 * (step - 1) + low],
            device_id=gy.at(gy.after(step)), device_id_type=MESH)

    def leave_quarter(quarter):
        low, half = quarter // 2, quarter % 2
        crossing(quarter).wait_recv()
        factor = scale_of(core_in.at[quarter], 2048)
        for i in range(8):
            mine[quarter, i // 4, i % 4] += wide(core_in[quarter, i * 256:i * 256 + 256, :]) * factor
        if half == 0:
            for high in range(2):
                to = high * 2 + low

                @pl.when(to != x)
                def _(high=high, to=to):
                    slot = lax.rem(to + 3 - x, 4)
                    code([summed(quarter, high, t) for t in range(4)], x_out.at[slot])
                    x_copy(to, slot).start()
        else:
            for step in (2, 1, 3):
                code([summed(quarter, t, gy.after(step)) for t in range(2)], y_out.at[step - 1, low])
                y_copy(step, low).start()

    def cross_quarter(quarter):
        result = products(1 - core, quarter)
        for i in range(8):
            apart[i] = result[:, i * 128:i * 128 + 128]
        code([lambda i=i: apart[i] for i in range(8)], theirs.at[quarter])
        crossing(quarter).start()

    def own_quarter(quarter):
        result = products(core, quarter)
        for i in range(8):
            mine[quarter, i // 4, i % 4] = result[:, i * 128:i * 128 + 128]

    cross_quarter(0)
    own_quarter(0)
    for quarter in range(1, 4):
        cross_quarter(quarter)
        leave_quarter(quarter - 1)
        own_quarter(quarter)
    leave_quarter(3)

    for slot in range(3):
        x_copy(gx.after(slot + 1), slot).wait_recv()
    for t in range(4):
        value = summed(2 * x_lo, x_hi, t)()
        for i in range(3):
            value += wide(x_in[i, t * 256:t * 256 + 256, :]) * scale_of(x_in.at[i], 1024)
        u[t] = value
    for step in range(1, 4):
        code([lambda: u[gy.after(step)]], y_out_2.at[step - 1])
    y_last = send(gy, lambda i: y_out_2.at[lax.rem(i + 3 - y, 4)], lambda i, s: y_in_2.at[s - 1])
    for step in range(1, 4):
        for low in range(2):
            y_copy(step, low).wait_recv()
    for t in range(4):
        value = summed(2 * (t % 2) + 1, t // 2, y)()
        for i in range(3):
            slot = y_in.at[i, t % 2]
            value += wide(y_in[i, t % 2, (t // 2) * 256:(t // 2) * 256 + 256, :]) * scale_of(slot, 512)
        v[t] = value
    for step in range(1, 4):
        code([lambda: v[gx.after(step)]], x_out_2.at[step - 1])
    x_last = send(gx, lambda i: x_out_2.at[lax.rem(i + 3 - x, 4)], lambda i, s: x_in_2.at[s - 1])
    arrived(y_last)
    value = u[y]
    for i in range(3):
        value += decode(y_in_2.at[i], 256)
    z_sum[0:256, :] = value
    arrived(x_last)
    value = v[x]
    for i in range(3):
        value += decode(x_in_2.at[i], 256)
    z_sum[256:512, :] = value

    def slab(i):
        return z_sum[pl.ds(pl.multiple_of(i * 64, 64), 64), :]

    for step in range(1, 8):
        code([lambda: slab(gz.after(step))], z_out.at[step - 1])
    to_z = send(gz, lambda i: z_out.at[lax.rem(i + 7 - z, 8)], lambda i, s: z_in.at[s - 1])
    first = full[0].reshape(1024, 1024)
    lengths = [
        jnp.transpose(jnp.broadcast_to(squares_of(full[0, t // 4, t % 4].reshape(128, 1024)), (128, 128)))[0:1, :]
        for t in range(8)
    ]
    lengths = jnp.concatenate(lengths, axis=1)
    for t in range(4):
        rows = full[1, t // 2, (t % 2) * 2:(t % 2) * 2 + 2].reshape(256, 1024)
        inner = lax.dot_general(rows, first, NT, **DOTS)
        high, low = halves(jnp.exp(-(squares_of(rows) + lengths - 2.0 * inner) * (0.5 / 1024)))
        near_high[t * 256:t * 256 + 256, :] = high
        near_low[t * 256:t * 256 + 256, :] = low

    left = lax.broadcasted_iota(jnp.int32, (64, 128), 1) < 64
    wanted_in[gr.me] = wanted[gr.me]
    arrived(wanted_sent)
    goal = jnp.where(left, decode(wanted_in[owner[0]], 64), decode(wanted_in[owner[1]], 64))
    arrived(to_z)
    value = slab(z)
    for i in range(7):
        value += decode(z_in.at[i], 64)
    residual = goal - value

    def spread(group, slots, value):
        code([lambda: value], slots.at[group.me])
        return send(group, lambda i: slots.at[group.me], lambda i, s: slots.at[i])

    def flip(value):
        return pltpu.roll(value, 64, 1)

    copies = spread(kinds["col"], res_all, residual)
    arrived(inverse_spread)
    rows_here = inverse_all[...].reshape(128, 1024)
    high, low = halves(rows_here)
    across = lax.dot_general(jnp.concatenate([high, low], axis=0), near_high[...], NN, **DOTS)
    linked[...] = across[0:128] + across[128:256] + lax.dot_general(high, near_low[...], NN, **DOTS)
    arrived(copies)
    for t in range(8):
        even, odd = decode(res_all.at[2 * t], 64), decode(res_all.at[2 * t + 1], 64)
        res[0, :, t * 128:t * 128 + 128] = jnp.where(left, even, flip(odd))
        res[1, :, t * 128:t * 128 + 128] = jnp.where(left, flip(even), odd)
    change_1 = lax.dot_general(res[0], rows_here, NT, precision=lax.Precision.HIGHEST, **DOTS)
    copies = spread(kinds["col"], delta_all, change_1)
    change_2 = lax.dot_general(res[1], rows_here, NT, precision=lax.Precision.HIGHEST, **DOTS)
    arrived(copies)
    for t in range(8):
        even, odd = decode(delta_all.at[2 * t], 64), decode(delta_all.at[2 * t + 1], 64)
        delta[:, t * 128:t * 128 + 128] = jnp.where(left, even, flip(odd))
    change_2 -= lax.dot_general(delta[...], linked[...], NT, precision=lax.Precision.HIGHEST, **DOTS)
    copies = spread(gr, last_all, jnp.where(left, change_1, change_2))
    arrived(copies)
    for t in range(8):
        value = jnp.concatenate([decode(last_all.at[2 * t], 64), decode(last_all.at[2 * t + 1], 64)], axis=0)
        lanes = min(128, classes - t * 128)
        value = jnp.transpose(value)
        out_1[:, t * 128:t * 128 + lanes] = value[0:64, 0:lanes]
        out_2[:, t * 128:t * 128 + lanes] = value[64:128, 0:lanes]
    for copies in started:
        sent(copies)

    for slot in range(3):
        x_copy(gx.after(slot + 1), slot).wait_send()
    for step in range(1, 4):
        for low in range(2):
            y_copy(step, low).wait_send()
    for quarter in range(4):
        crossing(quarter).wait_send()


def main(order, points, targets, coeffs, block_inverse, collective_id):
    i16, bf16 = jnp.int16, jnp.bfloat16
    return pl.pallas_call(
        main_kernel,
        out_shape=[jax.ShapeDtypeStruct((64, coeffs.shape[2]), F32)] * 2 + [jax.ShapeDtypeStruct((16, 128), F32)],
        in_specs=[pl.BlockSpec(memory_space=pltpu.SMEM), ANY, ANY, ANY, ANY],
        out_specs=[VMEM] * 3,
        scratch_shapes=[
            pltpu.VMEM(points.shape, bf16),
            pltpu.VMEM(targets.shape, bf16),
            pltpu.VMEM(coeffs.shape, F32),
            pltpu.VMEM(block_inverse.shape, F32),
            pltpu.VMEM((16, 16, 512), bf16),
            pltpu.VMEM((16, 8, 1024), F32),
            pltpu.VMEM((16, 16, 512), bf16),
            pltpu.VMEM((16, 512), bf16),
            pltpu.VMEM((2, 2, 4, 2, 2, 32, 1024), bf16),
            pltpu.VMEM((1024, 1152), bf16),
            pltpu.VMEM((8, 384), F32),
            pltpu.VMEM((2, 4, 256, 1152), bf16),
            pltpu.VMEM((4, 2, 4, 256, 128), F32),
            pltpu.VMEM((8, 256, 128), F32),
            pltpu.VMEM((4, 2064, 128), i16),
            pltpu.VMEM((4, 2064, 128), i16),
            pltpu.VMEM((3, 1040, 128), i16),
            pltpu.VMEM((3, 1040, 128), i16),
            pltpu.VMEM((3, 2, 528, 128), i16),
            pltpu.VMEM((3, 2, 528, 128), i16),
            pltpu.VMEM((4, 256, 128), F32),
            pltpu.VMEM((4, 256, 128), F32),
            pltpu.VMEM((3, 272, 128), i16),
            pltpu.VMEM((3, 272, 128), i16),
            pltpu.VMEM((3, 272, 128), i16),
            pltpu.VMEM((3, 272, 128), i16),
            pltpu.VMEM((512, 128), F32),
            pltpu.VMEM((7, 80, 128), i16),
            pltpu.VMEM((7, 80, 128), i16),
            pltpu.VMEM((16, 8, 1024), F32),
            pltpu.VMEM((16, 8, 1024), F32),
            pltpu.VMEM((16, 80, 128), i16),
            pltpu.VMEM((16, 80, 128), i16),
            pltpu.VMEM((16, 80, 128), i16),
            pltpu.VMEM((16, 80, 128), i16),
            pltpu.VMEM((16, 80, 128), i16),
            pltpu.VMEM((2, 64, 1024), F32),
            pltpu.VMEM((64, 1024), F32),
            pltpu.VMEM((1024, 1024), bf16),
            pltpu.VMEM((1024, 1024), bf16),
            pltpu.VMEM((128, 1024), F32),
            DMA((160,)), DMA((160,)), DMA((4,)), DMA((4,)),
        ],
        compiler_params=pltpu.CompilerParams(collective_id=collective_id, has_side_effects=True, vmem_limit_bytes=56 * 2**20),
    )(order, points, targets, coeffs, block_inverse)


def on_device(points, targets, coeffs, block_inverse, block_order):
    blocks_here = points.shape[0]
    change_1, change_2, hit = main(block_order, points, targets, coeffs, block_inverse, 0)
    hit = hit.reshape(2, 8, 128)[:, :blocks_here, 0:1, None] > 0
    return jnp.where(hit[0], coeffs + change_1[None], jnp.where(hit[1], coeffs + change_2[None], coeffs))


def solution(mesh):
    placed = (
        P("row", "col", None),
        P("row", "col", None),
        P("row", "col", None),
        P("row", "col", None),
        P(),
    )
    return jax.shard_map(
        on_device, mesh=mesh, in_specs=placed, out_specs=P("row", "col", None), check_vma=False
    )
```
